128 devices in a mesh: gx: 16 (over y, z), gy: 8 (over x, core).
Axes of the slice: x: 4, y: 4, z: 4, core: 2. Of those that a mesh axis runs over, the one named last changes fastest.
Arguments:
- inputs: float32 [2, 128, 8192], P(None, 'gy', 'gx'), may hold values from -56 to 56
- positions: int32 [128], P(('gx', 'gy')), may hold values from 1024 to 4095
- attn_gain: float32 [8192], P('gx'), may hold values from 0.5 to 1.5
- ffn_gain: float32 [8192], P('gx'), may hold values from 0.5 to 1.5
- qkv_weight: bfloat16 [8192, 10240], P('gx', 'gy'), may hold values from -0.0625 to 0.0625
- out_weight: bfloat16 [8192, 8192], P('gy', 'gx'), may hold values from -0.0625 to 0.0625
- gate_weight: bfloat16 [8192, 28672], P('gx', 'gy'), may hold values from -0.0625 to 0.0625
- up_weight: bfloat16 [8192, 28672], P('gx', 'gy'), may hold values from -0.0625 to 0.0625
- down_weight: bfloat16 [28672, 8192], P('gy', 'gx'), may hold values from -0.03125 to 0.03125
- k_cache: bfloat16 [128, 8, 1024, 128], P(('gx', 'gy')), may hold values from -400 to 400
- v_cache: bfloat16 [128, 8, 1024, 128], P(('gx', 'gy')), may hold values from -12 to 12
Outputs:
- outputs: float32 [2, 128, 8192], P(None, 'gy', 'gx')
- new_kv: bfloat16 [128, 2, 8, 256], P(('gx', 'gy'))
The draws below stay inside these ranges and needn't reach their ends.
All inputs are finite; a program needn't handle non-finite values.
Results may differ from the reference program's by a relative error of at most 0.0065.
Values may be sent and summed in bfloat16 or wider, within the bound.
No kernel may reach another device: no remote copies, remote signals or barrier semaphores. Data moves between devices by JAX's collectives and lax.ppermute only.
A program may use at most 128 MiB of HBM per device.

```python
import jax
import jax.numpy as jnp
from jax import lax

D = 8192
FF = 28672
NH = 64
KVH = 8
HD = 128
CACHE = 1024
GQ = 8
QKV = 10240
ROWS = 128


def draw_inputs(key, part):
    key = jax.random.fold_in(key, 11)
    key_base, key_rows, key_cols = jax.random.split(key, 3)
    column = jnp.arange(D, dtype=jnp.float32) / D
    random_part = jnp.clip(jax.random.normal(key_base, (2, ROWS, D), jnp.float32), -4.0, 4.0)
    rising = jnp.exp(column * jnp.log(3.0))
    row_scale = jnp.exp(jax.random.uniform(key_rows, (2, ROWS, 1), jnp.float32, jnp.log(0.5), jnp.log(2.0)))
    column_scale = jnp.exp(jax.random.uniform(key_cols, (D,), jnp.float32, jnp.log(0.6), jnp.log(1.8)))
    return random_part * row_scale * column_scale * rising


def draw_k_cache(key, part):
    key = jax.random.fold_in(key, 23)
    key_main = jax.random.fold_in(key, 0)
    values = jnp.clip(jax.random.normal(key_main, (ROWS, KVH, CACHE, HD), jnp.float32), -4.0, 4.0)
    scaled = values * 2.5
    return scaled.astype(jnp.bfloat16)


def with_ends(drawn, rng, smallest, largest):
    extent = drawn.shape
    place = [jax.random.randint(jax.random.fold_in(rng, axis), (), 0, extent[axis]) for axis in range(len(extent))]
    drawn = drawn.at[tuple(place)].set(smallest)
    longest = extent.index(max(extent))
    place[longest] = (place[longest] + 1) % extent[longest]
    return drawn.at[tuple(place)].set(largest)


def shard_levels(rng, dims, cuts, low, largest):
    loudness = 1.0
    for position, shards_of in cuts:
        heights = jax.random.uniform(jax.random.fold_in(jax.random.fold_in(rng, 6), position), (shards_of,), jnp.float32, low / len(cuts), largest / len(cuts))
        loudness = loudness * jnp.repeat(jnp.exp(heights), dims[position] // shards_of).reshape((-1,) + (1,) * (len(dims) - 1 - position))
    return loudness


def gaussian(rng, shape, scale, most, cuts=(), kind=jnp.bfloat16):
    result = scale * jax.random.normal(rng, shape, jnp.float32)
    if cuts:
        result = result * shard_levels(rng, shape, cuts, -0.22, 0.18)
    return jnp.clip(result, -most, most).astype(kind)


def setup_inputs(seed: int = 0) -> dict:
    seeds = jax.random.split(jax.random.key(seed), 12)
    return {
        "inputs": draw_inputs(jax.random.fold_in(seeds[11], 71), 0),
        "positions": with_ends(jax.random.randint(seeds[1], (ROWS,), CACHE, 4 * CACHE), jax.random.fold_in(seeds[1], 1), CACHE, (4 * CACHE) - 1).astype(jnp.int32),
        "attn_gain": jnp.clip(1.0 + 0.1 * jax.random.normal(seeds[2], (D,), jnp.float32), 0.5, 1.5),
        "ffn_gain": jnp.clip(1.0 + 0.1 * jax.random.normal(seeds[3], (D,), jnp.float32), 0.5, 1.5),
        "qkv_weight": gaussian(seeds[4], (D, QKV), D ** -0.5, 0.0625, ((0, 16), (1, 8))),
        "out_weight": gaussian(seeds[5], (NH * HD, D), (NH * HD) ** -0.5, 0.0625, ((0, 8), (1, 16))),
        "gate_weight": gaussian(seeds[6], (D, FF), D ** -0.5, 0.0625, ((0, 16), (1, 8))),
        "up_weight": gaussian(seeds[7], (D, FF), D ** -0.5, 0.0625, ((0, 16), (1, 8))),
        "down_weight": gaussian(seeds[8], (FF, D), FF ** -0.5, 0.03125, ((0, 8), (1, 16))),
        "k_cache": draw_k_cache(jax.random.fold_in(seeds[11], 71), 0),
        "v_cache": gaussian(seeds[10], (ROWS, KVH, CACHE, HD), 3.0, 12.0, ((0, 128),)),
    }


EPSILON = 1e-05
THETA = 500000.0

def rotate(vectors, angle_pos):
    half_size = vectors.shape[-1] // 2
    frequency = jnp.exp(jnp.arange(half_size, dtype=jnp.float32) * (-2.0 / vectors.shape[-1]) * jnp.log(THETA))
    angles = angle_pos[..., None] * frequency
    cosine = jnp.cos(angles)
    sine_part = jnp.sin(angles)
    first_half = vectors[..., :half_size]
    second_half = vectors[..., half_size:]
    return jnp.concatenate([first_half * cosine - second_half * sine_part, second_half * cosine + first_half * sine_part], -1)

def normalize(residual, gain):
    mean_square = lax.optimization_barrier(jnp.mean(residual * residual, axis=-1, keepdims=True))
    return (residual * lax.rsqrt(mean_square + EPSILON) * gain).astype(jnp.bfloat16)

def attend_group(queries, key_cache, value_cache, fresh_keys, fresh_values):
    cache_scores = jnp.einsum('rhd,rcd->rhc', queries.astype(jnp.float32), key_cache.astype(jnp.float32))
    fresh_scores = jnp.einsum('rhd,rsd->rhs', queries.astype(jnp.float32), fresh_keys.astype(jnp.float32))
    row_top = jnp.maximum(lax.optimization_barrier(jnp.max(cache_scores, -1)), lax.optimization_barrier(jnp.max(fresh_scores, -1)))[..., None]
    cache_exp = jnp.exp(cache_scores - row_top)
    fresh_exp = jnp.exp(fresh_scores - row_top)
    row_total = lax.optimization_barrier(jnp.sum(cache_exp, -1, keepdims=True)) + lax.optimization_barrier(jnp.sum(fresh_exp, -1, keepdims=True))
    cache_probs = (cache_exp / row_total).astype(jnp.bfloat16)
    fresh_probs = (fresh_exp / row_total).astype(jnp.bfloat16)
    mixed_out = jnp.einsum('rhc,rcd->rhd', cache_probs.astype(jnp.float32), value_cache.astype(jnp.float32))
    return mixed_out + jnp.einsum('rhs,rsd->rhd', fresh_probs.astype(jnp.float32), fresh_values.astype(jnp.float32))

def reference(inputs, positions, attn_gain, ffn_gain, qkv_weight, out_weight, gate_weight, up_weight, down_weight, k_cache, v_cache):
    fresh_k = []
    fresh_v = []
    results = []
    kv_steps = []
    for step_index in range(2):
        residual = inputs[step_index]
        normed = normalize(residual, attn_gain)
        qkv = jnp.dot(normed, qkv_weight, preferred_element_type=jnp.float32).astype(jnp.bfloat16)
        qkv = qkv.reshape(ROWS, KVH, GQ + 2, HD)
        angle_pos = (positions + step_index).astype(jnp.float32)
        queries = (rotate(qkv[:, :, :GQ].astype(jnp.float32), angle_pos[:, None, None]) * HD ** (-0.5)).astype(jnp.bfloat16)
        key_now = rotate(qkv[:, :, GQ].astype(jnp.float32), angle_pos[:, None]).astype(jnp.bfloat16)
        value_now = qkv[:, :, GQ + 1]
        fresh_k.append(key_now)
        fresh_v.append(value_now)
        kv_steps.append(jnp.concatenate([key_now, value_now], -1))
        stacked_keys = jnp.stack(fresh_k, 2)
        stacked_values = jnp.stack(fresh_v, 2)

        def one_group(group):

            def fetch(tensor):
                return lax.dynamic_index_in_dim(tensor, group, 1, keepdims=False)
            return attend_group(fetch(queries), fetch(k_cache), fetch(v_cache), fetch(stacked_keys), fetch(stacked_values))
        grouped = lax.map(one_group, jnp.arange(KVH, dtype=jnp.int32))
        attended = jnp.transpose(grouped, (1, 0, 2, 3)).reshape(ROWS, NH * HD).astype(jnp.bfloat16)
        after_attn = residual + jnp.dot(attended, out_weight, preferred_element_type=jnp.float32)
        normed_ffn = normalize(after_attn, ffn_gain)
        gate_part = jnp.dot(normed_ffn, gate_weight, preferred_element_type=jnp.float32)
        up_part = jnp.dot(normed_ffn, up_weight, preferred_element_type=jnp.float32)
        hidden = (jax.nn.silu(gate_part) * up_part).astype(jnp.bfloat16)
        results.append(after_attn + jnp.dot(hidden, down_weight, preferred_element_type=jnp.float32))
    return (jnp.stack(results, 0), jnp.stack(kv_steps, 1))
```

```python
import functools

import jax
import jax.numpy as jnp
from jax import lax
from jax.experimental import pallas as pl
from jax.experimental.pallas import tpu as pltpu
from jax.sharding import PartitionSpec as P

D = 8192
KVH = 8
HD = 128
CACHE = 1024
GQ = 8
EPSILON = 1e-05
THETA = 500000.0
NX = 16
NY = 8
WIDTH = 512
UNITS = 3584
FLOWS = 4
FW = UNITS // FLOWS
F32 = jnp.float32
BF16 = jnp.bfloat16
MIB = 1 << 20

VM = pl.BlockSpec(memory_space=pltpu.VMEM)
SM = pl.BlockSpec(memory_space=pltpu.SMEM)
ANY = pl.BlockSpec(memory_space=pl.ANY)


def swap_gx(array, bits):
    return lax.ppermute(array, "gx", [(i, i ^ bits) for i in range(NX)])


def swap_gy(array, bits):
    return lax.ppermute(array, "gy", [(i, i ^ bits) for i in range(NY)])


def gray(place):
    return ((place & 1) ^ (place >> 1)) * 2 + (place >> 1)


def call(body, outs, ins, scratch=(), limit=32):
    return pl.pallas_call(
        body,
        out_shape=outs,
        in_specs=ins,
        out_specs=jax.tree.map(lambda _: VM, outs),
        scratch_shapes=list(scratch),
        compiler_params=pltpu.CompilerParams(vmem_limit_bytes=limit * MIB),
    )


def shaped(shape, dtype):
    return jax.ShapeDtypeStruct(shape, dtype)


def qkv_body(where, near, far, gain, weight, out, lhs, rows, held, sem):
    fetch = pltpu.make_async_copy(weight, held, sem)
    fetch.start()
    mine = where[1]
    for flag, source in enumerate((near, far)):
        for k in range(4):
            block = mine ^ (2 * k + flag)
            for t in range(2):
                start = pl.multiple_of(t * 128 + block * 16, 16)
                lhs[pl.ds(start, 16), :] = source[k * 32 + t * 16 : k * 32 + t * 16 + 16, :]
    plain = lhs[...].astype(F32) / gain[...]
    squares = jnp.sum(plain * plain, axis=1, keepdims=True)
    for t in range(2):
        whole = jnp.broadcast_to(squares[t * 128 : t * 128 + 128], (128, HD))
        high = whole.astype(BF16).astype(F32)
        rows[pl.ds(20 + 2 * t, 128, stride=24), :] = high
        rows[pl.ds(21 + 2 * t, 128, stride=24), :] = whole - high
    fetch.wait()
    for pair in range(5):
        part = jnp.dot(lhs[...], held[:, pair * 256 : pair * 256 + 256], preferred_element_type=F32)
        for j in (2 * pair, 2 * pair + 1):
            for t in range(2):
                place = t * 8 + j if j < GQ else 16 + (j - GQ) * 2 + t
                column = (j - 2 * pair) * HD
                rows[pl.ds(place, 128, stride=24), :] = part[t * 128 : t * 128 + 128, column : column + HD]
    out[...] = rows[...].astype(BF16)


def qkv_partial(where, near, far, gain, weight):
    return call(
        qkv_body,
        shaped((128 * 24, HD), BF16),
        [SM, VM, VM, VM, ANY],
        [
            pltpu.VMEM((256, WIDTH), BF16),
            pltpu.VMEM((128 * 24, HD), F32),
            pltpu.VMEM((WIDTH, 1280), BF16),
            pltpu.SemaphoreType.DMA,
        ],
    )(where, near, far, gain, weight)


def turn(vectors, cosine, sine):
    return vectors * cosine + pltpu.roll(vectors, HD // 2, vectors.ndim - 1) * sine


def attend_body(angles, received, keys, values, out, fresh, scores, held_k, held_v, sem_k, sem_v):
    fetches = []
    for g in range(KVH):
        for cache, held, sem in ((keys, held_k, sem_k), (values, held_v, sem_v)):
            fetch = pltpu.make_async_copy(cache.at[0, g], held.at[g], sem.at[g])
            fetch.start()
            fetches.append(fetch)
    total = received[0].astype(F32)
    for i in range(1, NX):
        total = total + received[i].astype(F32)
    squares = total[:, 20:24, :]
    scales = []
    for t in range(2):
        square = squares[:, 2 * t : 2 * t + 1, :] + squares[:, 2 * t + 1 : 2 * t + 2, :]
        scales.append(lax.rsqrt(square / D + EPSILON))
    cosines = [angles[2 * t : 2 * t + 1, :] for t in range(2)]
    sines = [angles[2 * t + 1 : 2 * t + 2, :] for t in range(2)]
    queries, new_keys, new_values = [], [], []
    for t in range(2):
        head = (total[:, 8 * t : 8 * t + 8, :] * scales[t]).astype(BF16).astype(F32)
        flat = turn(head.reshape(64, HD), cosines[t], sines[t])
        queries.append((flat * HD**-0.5).astype(BF16).astype(F32).reshape(8, 8, HD))
        key = (total[:, 16 + t : 17 + t, :] * scales[t]).astype(BF16).astype(F32).reshape(8, HD)
        new_keys.append(turn(key, cosines[t], sines[t]).astype(BF16))
        value = (total[:, 18 + t : 19 + t, :] * scales[t]).astype(BF16).reshape(8, HD)
        new_values.append(value)
        fresh[0, t, :, :HD] = new_keys[t]
        fresh[0, t, :, HD:] = value
    both = jnp.concatenate(queries, axis=1)
    both16 = both.astype(BF16)
    for g in range(KVH):
        fetches[2 * g].wait()
        scores[g * 16 : g * 16 + 16, :] = lax.dot_general(
            both16[g], held_k[g], (((1,), (1,)), ((), ())), preferred_element_type=F32
        )
    extra = []
    step = lax.broadcasted_iota(jnp.int32, (KVH, 16, 1), 1) // GQ
    for t in range(2):
        dots = jnp.sum(both * new_keys[t].astype(F32).reshape(KVH, 1, HD), axis=2, keepdims=True)
        if t == 1:
            dots = jnp.where(step >= 1, dots, -3.0e38)
        extra.append(dots.reshape(128, 1))
    cached = scores[...]
    top = jnp.maximum(jnp.max(cached, axis=1, keepdims=True), jnp.maximum(extra[0], extra[1]))
    cached = jnp.exp(cached - top)
    extra = [jnp.exp(value - top) for value in extra]
    share = 1.0 / (jnp.sum(cached, axis=1, keepdims=True) + extra[0] + extra[1])
    probs = (cached * share).astype(BF16)
    extra = [(value * share).astype(BF16).astype(F32).reshape(KVH, 16, 1) for value in extra]
    for g in range(KVH):
        fetches[2 * g + 1].wait()
        mixed = jnp.dot(probs[g * 16 : g * 16 + 16, :], held_v[g], preferred_element_type=F32)
        for t in range(2):
            mixed = mixed + extra[t][g] * new_values[t][g : g + 1, :].astype(F32)
        mixed = mixed.astype(BF16)
        for i in range(NX):
            out[i, g] = mixed


def attend(angles, received, keys, values):
    return call(
        attend_body,
        (shaped((NX, KVH, 16, HD), BF16), shaped((1, 2, KVH, 2 * HD), BF16)),
        [VM, VM, ANY, ANY],
        [
            pltpu.VMEM((KVH * 16, CACHE), F32),
            pltpu.VMEM((KVH, CACHE, HD), BF16),
            pltpu.VMEM((KVH, CACHE, HD), BF16),
            pltpu.SemaphoreType.DMA((KVH,)),
            pltpu.SemaphoreType.DMA((KVH,)),
        ],
    )(angles, received, keys, values)


def out_body(where, received, weight, keep, send, wide, lhs, held, sem):
    fetch = pltpu.make_async_copy(weight, held, sem)
    fetch.start()
    mine = where[1]
    wide[...] = received[...].astype(F32)
    for flag in range(2):
        for k in range(4):
            block = mine ^ (2 * k + flag)
            for t in range(2):
                place = flag * 128 + k * 32 + t * 16
                for h in range(GQ):
                    start = block * 256 + t * 8 + h
                    lhs[place : place + 16, h * HD : h * HD + HD] = wide[
                        pl.ds(start, 16, stride=16), :
                    ].astype(BF16)
    fetch.wait()
    keep[...] = jnp.dot(lhs[:128, :], held[...], preferred_element_type=F32)
    send[...] = jnp.dot(lhs[128:, :], held[...], preferred_element_type=F32).astype(BF16)


def out_partial(where, received, weight):
    return call(
        out_body,
        (shaped((128, WIDTH), F32), shaped((128, WIDTH), BF16)),
        [SM, VM, ANY],
        [
            pltpu.VMEM((128 * 16, HD), F32),
            pltpu.VMEM((256, KVH * HD), BF16),
            pltpu.VMEM((KVH * HD, WIDTH), BF16),
            pltpu.SemaphoreType.DMA,
        ],
    )(where, received, weight)


def split_body(keep, other, own, *sends):
    whole = keep[...] + other[...].astype(F32)
    own[...] = whole[:32]
    for k, send in enumerate(sends):
        send[...] = whole[32 * k + 32 : 32 * k + 64].astype(BF16)


def sum_over_gy(keep, send):
    other = swap_gy(send, 1)
    own, *sends = call(
        split_body,
        (shaped((32, WIDTH), F32),) + (shaped((32, WIDTH), BF16),) * 3,
        [VM, VM],
    )(keep, other)
    return [own] + [swap_gy(piece, 2 * (k + 1)) for k, piece in enumerate(sends)]


def residual_body(residual, gain, own, one, two, three, after, normed):
    whole = residual[...] + (own[...] + one[...].astype(F32) + two[...].astype(F32) + three[...].astype(F32))
    after[...] = whole
    normed[...] = (whole * gain[...]).astype(BF16)


def final_body(residual, own, one, two, three, out):
    out[...] = residual[...] + (own[...] + one[...].astype(F32) + two[...].astype(F32) + three[...].astype(F32))


def stack_body(*refs):
    *pieces, out = refs
    rows = pieces[0].shape[0]
    for k, piece in enumerate(pieces):
        out[k * rows : k * rows + rows, :] = piece[...]


def gather_gy(own):
    pieces = [own] + [swap_gy(own, 2 * k) for k in (1, 2, 3)]
    near = call(stack_body, shaped((128, WIDTH), BF16), [VM] * 4)(*pieces)
    return near, swap_gy(near, 1)


def rotate_left(value, by):
    return ((value << by) | (value >> (4 - by))) & 15 if by else value


def widths():
    return [2 * FW + (HD if f == 0 else 0) for f in range(FLOWS)]


def gate_body(where, near, far, gain, gate, up, *refs):
    outs, (lhs, held, sem) = refs[: 2 * FLOWS], refs[2 * FLOWS :]
    fetches = []
    for f in range(FLOWS):
        for i, weight in enumerate((gate, up)):
            fetch = pltpu.make_async_copy(weight.at[:, pl.ds(f * FW, FW)], held.at[f, i], sem.at[f, i])
            fetch.start()
            fetches.append(fetch)
    for f in range(FLOWS):
        for flag, source in enumerate((near, far)):
            for k in range(4):
                block = where[1] ^ (2 * k + flag)
                for t in range(2):
                    place = rotate_left((2 * block + t) ^ where[0], f)
                    start = pl.multiple_of(place * 16, 16)
                    lhs[f, pl.ds(start, 16), :] = source[k * 32 + t * 16 : k * 32 + t * 16 + 16, :]
    for f in range(FLOWS):
        keep, send = outs[2 * f], outs[2 * f + 1]
        if f == 0:
            plain = lhs[0].astype(F32) / gain[...]
            squares = jnp.sum(plain * plain, axis=1, keepdims=True)
            keep[:, 2 * FW :] = jnp.broadcast_to(squares[:128], (128, HD))
            send[:, 2 * FW :] = two_parts(jnp.broadcast_to(squares[128:], (128, HD)))
        for i in range(2):
            fetches[2 * f + i].wait()
            columns = slice(i * FW, i * FW + FW)
            keep[:, columns] = jnp.dot(lhs[f, :128, :], held[f, i], preferred_element_type=F32)
            send[:, columns] = jnp.dot(lhs[f, 128:, :], held[f, i], preferred_element_type=F32).astype(BF16)


def two_parts(squares):
    high = squares.astype(BF16).astype(F32)
    first = lax.broadcasted_iota(jnp.int32, squares.shape, 1) < HD // 2
    return jnp.where(first, high, squares - high).astype(BF16)


def one_part(parts):
    wide = parts.astype(F32)
    return wide + pltpu.roll(wide, HD // 2, 1)


def gate_partial(where, near, far, gain, gate, up):
    outs = []
    for width in widths():
        outs += [shaped((128, width), F32), shaped((128, width), BF16)]
    return call(
        gate_body,
        tuple(outs),
        [SM, VM, VM, VM, ANY, ANY],
        [
            pltpu.VMEM((FLOWS, 256, WIDTH), BF16),
            pltpu.VMEM((FLOWS, 2, WIDTH, FW), BF16),
            pltpu.SemaphoreType.DMA((FLOWS, 2)),
        ],
        limit=40,
    )(where, near, far, gain, gate, up)


def halve_body(*refs):
    ins, outs = refs[: 2 * FLOWS], refs[2 * FLOWS :]
    for f in range(FLOWS):
        keep, other = ins[2 * f], ins[2 * f + 1]
        half = keep.shape[0] // 2
        whole = keep[:, : 2 * FW] + other[:, : 2 * FW].astype(F32)
        outs[2 * f][:, : 2 * FW] = whole[:half]
        outs[2 * f + 1][:, : 2 * FW] = whole[half:].astype(BF16)
        if f == 0:
            squares = keep[:, 2 * FW :] + one_part(other[:, 2 * FW :])
            outs[0][:, 2 * FW :] = squares[:half]
            outs[1][:, 2 * FW :] = two_parts(squares[half:])


def hidden_body(*refs):
    ins, outs = refs[: 2 * FLOWS], refs[2 * FLOWS :]
    squares = ins[0][:, 2 * FW :] + one_part(ins[1][:, 2 * FW :])
    scale = lax.rsqrt(squares / D + EPSILON)[:, :1]
    for f in range(FLOWS):
        whole = (ins[2 * f][:, : 2 * FW] + ins[2 * f + 1][:, : 2 * FW].astype(F32)) * scale
        gate, up = whole[:, :FW], whole[:, FW:]
        units = (gate / (1.0 + jnp.exp(-gate)) * up).astype(BF16)
        outs[f // 2][:, (f % 2) * FW : (f % 2) * FW + FW] = units


def hidden_units(where, near, far, gain, gate, up):
    parts = gate_partial(where, near, far, gain, gate, up)
    steps = (4, 12, 1, 3)
    rows = 128
    for step in range(4):
        moved = list(parts)
        for f in range(FLOWS):
            moved[2 * f + 1] = swap_gx(parts[2 * f + 1], steps[(step + f) % 4])
        if step == 3:
            break
        rows //= 2
        outs = []
        for width in widths():
            outs += [shaped((rows, width), F32), shaped((rows, width), BF16)]
        parts = call(halve_body, tuple(outs), [VM] * (2 * FLOWS))(*moved)
    return call(hidden_body, (shaped((16, 2 * FW), BF16),) * 2, [VM] * (2 * FLOWS))(*moved)


def stack_two_body(*refs):
    ins, outs = refs[:8], refs[8:]
    for side in range(2):
        for k in range(4):
            outs[side][k * 16 : k * 16 + 16, :] = ins[4 * side + k][...]


def down_body(where, *refs):
    pieces, (weight, keep, send, lhs, held, sem) = refs[:8], refs[8:]
    half = 2 * FW
    fetches = []
    for side in range(2):
        fetch = pltpu.make_async_copy(weight.at[pl.ds(side * half, half)], held.at[side], sem.at[side])
        fetch.start()
        fetches.append(fetch)
    for side in range(2):
        for m in range(4):
            for k in range(4):
                y, z = (k, m) if side == 0 else (m, k)
                place = where[0] ^ (gray(y) * 4 + gray(z))
                block = (place >> 1) ^ where[1]
                start = (block & 1) * 128 + (block >> 1) * 32 + (place & 1) * 16
                start = pl.multiple_of(start, 16)
                lhs[side, pl.ds(start, 16), :] = pieces[4 * side + m][k * 16 : k * 16 + 16, :]
    for fetch in fetches:
        fetch.wait()
    keep[...] = jnp.dot(lhs[0, :128, :], held[0], preferred_element_type=F32) + jnp.dot(
        lhs[1, :128, :], held[1], preferred_element_type=F32
    )
    send[...] = (
        jnp.dot(lhs[0, 128:, :], held[0], preferred_element_type=F32)
        + jnp.dot(lhs[1, 128:, :], held[1], preferred_element_type=F32)
    ).astype(BF16)


def down_partial(where, units, weight):
    ups = [units[0]] + [swap_gx(units[0], 4 * k) for k in (1, 2, 3)]
    zs = [units[1]] + [swap_gx(units[1], k) for k in (1, 2, 3)]
    first, second = call(stack_two_body, (shaped((64, 2 * FW), BF16),) * 2, [VM] * 8)(*ups, *zs)
    ups = [first] + [swap_gx(first, k) for k in (1, 2, 3)]
    zs = [second] + [swap_gx(second, 4 * k) for k in (1, 2, 3)]
    return call(
        down_body,
        (shaped((128, WIDTH), F32), shaped((128, WIDTH), BF16)),
        [SM] + [VM] * 8 + [ANY],
        [
            pltpu.VMEM((2, 256, 2 * FW), BF16),
            pltpu.VMEM((2, 2 * FW, WIDTH), BF16),
            pltpu.SemaphoreType.DMA((2,)),
        ],
    )(where, *ups, *zs, weight)


def rotations(positions):
    frequency = jnp.exp(jnp.arange(HD // 2, dtype=F32) * (-2.0 / HD) * jnp.log(THETA))
    rows = []
    for t in range(2):
        angles = (positions + t).astype(F32) * frequency
        cosine, sine = jnp.cos(angles), jnp.sin(angles)
        rows += [jnp.concatenate([cosine, cosine]), jnp.concatenate([-sine, sine])]
    return jnp.stack(rows)


def per_device(
    inputs,
    positions,
    attn_gain,
    ffn_gain,
    qkv_weight,
    out_weight,
    gate_weight,
    up_weight,
    down_weight,
    k_cache,
    v_cache,
):
    gx, gy = lax.axis_index("gx"), lax.axis_index("gy")
    where = jnp.stack([gray(gx >> 2) * 4 + gray(gx & 3), gy]).astype(jnp.int32)
    angles = rotations(positions)
    residual = inputs.reshape(32, WIDTH)
    attn_gain, ffn_gain = attn_gain.reshape(1, WIDTH), ffn_gain.reshape(1, WIDTH)

    near, far = gather_gy((residual * attn_gain).astype(BF16))
    partial = qkv_partial(where, near, far, attn_gain, qkv_weight).reshape(128, 24, HD)
    received = lax.all_to_all(partial, ("gx", "gy"), 0, 0, tiled=True).reshape(NX, NY, 24, HD)
    attended, new_kv = attend(angles, received, k_cache, v_cache)
    heads = lax.all_to_all(attended.reshape(128, 16, HD), ("gx", "gy"), 0, 0, tiled=True)
    pieces = sum_over_gy(*out_partial(where, heads.reshape(128 * 16, HD), out_weight))
    after_attn, normed = call(
        residual_body, (shaped((32, WIDTH), F32), shaped((32, WIDTH), BF16)), [VM] * 6
    )(residual, ffn_gain, *pieces)

    near, far = gather_gy(normed)
    units = hidden_units(where, near, far, ffn_gain, gate_weight, up_weight)
    pieces = sum_over_gy(*down_partial(where, units, down_weight))
    outputs = call(final_body, shaped((32, WIDTH), F32), [VM] * 5)(after_attn, *pieces)
    return outputs.reshape(2, 16, WIDTH), new_kv


def solution(mesh):
    placed = (
        P(None, "gy", "gx"),
        P(("gx", "gy")),
        P("gx"),
        P("gx"),
        P("gx", "gy"),
        P("gy", "gx"),
        P("gx", "gy"),
        P("gx", "gy"),
        P("gy", "gx"),
        P(("gx", "gy"), None, None, None),
        P(("gx", "gy"), None, None, None),
    )
    return jax.shard_map(
        per_device,
        mesh=mesh,
        in_specs=placed,
        out_specs=(P(None, "gy", "gx"), P(("gx", "gy"), None, None, None)),
        check_vma=False,
    )
```

```python
import functools

import jax
import jax.numpy as jnp
from jax import lax
from jax.experimental import pallas as pl
from jax.experimental.pallas import tpu as pltpu
from jax.sharding import PartitionSpec as P

D = 8192
KVH = 8
HD = 128
CACHE = 1024
GQ = 8
EPSILON = 1e-05
THETA = 500000.0
NX = 16
NY = 8
WIDTH = 512
UNITS = 3584
HALF = UNITS // 2
WIDTHS = (2 * HALF + HD, 2 * HALF)
F32 = jnp.float32
BF16 = jnp.bfloat16
MIB = 1 << 20

VM = pl.BlockSpec(memory_space=pltpu.VMEM)
SM = pl.BlockSpec(memory_space=pltpu.SMEM)
HBM = pl.BlockSpec(memory_space=pltpu.HBM)
DMA = pltpu.SemaphoreType.DMA


def swap_gx(array, bits):
    return lax.ppermute(array, "gx", [(i, i ^ bits) for i in range(NX)])


def swap_gy(array, bits):
    return lax.ppermute(array, "gy", [(i, i ^ bits) for i in range(NY)])


def gray(place):
    return ((place & 1) ^ (place >> 1)) * 2 + (place >> 1)


def call(body, outs, ins, scratch=(), limit=32):
    return pl.pallas_call(
        body,
        out_shape=outs,
        in_specs=ins,
        out_specs=jax.tree.map(lambda _: VM, outs),
        scratch_shapes=list(scratch),
        compiler_params=pltpu.CompilerParams(vmem_limit_bytes=limit * MIB),
    )


def hbm(array):
    return pltpu.with_memory_space_constraint(array, pltpu.HBM)


def shaped(shape, dtype):
    return jax.ShapeDtypeStruct(shape, dtype)


def qkv_body(where, near, far, gain, weight, out, lhs, rows, held, sem):
    fetch = pltpu.make_async_copy(weight, held, sem)
    fetch.start()
    mine = where[1]
    for flag, source in enumerate((near, far)):
        for k in range(4):
            block = mine ^ (2 * k + flag)
            for t in range(2):
                start = pl.multiple_of(t * 128 + block * 16, 16)
                lhs[pl.ds(start, 16), :] = source[k * 32 + t * 16 : k * 32 + t * 16 + 16, :]
    plain = lhs[...].astype(F32) / gain[...]
    squares = jnp.sum(plain * plain, axis=1, keepdims=True)
    for t in range(2):
        whole = jnp.broadcast_to(squares[t * 128 : t * 128 + 128], (128, HD))
        high = whole.astype(BF16).astype(F32)
        rows[pl.ds(20 + 2 * t, 128, stride=24), :] = high
        rows[pl.ds(21 + 2 * t, 128, stride=24), :] = whole - high
    fetch.wait()
    for pair in range(5):
        part = jnp.dot(lhs[...], held[:, pair * 256 : pair * 256 + 256], preferred_element_type=F32)
        for j in (2 * pair, 2 * pair + 1):
            for t in range(2):
                place = t * 8 + j if j < GQ else 16 + (j - GQ) * 2 + t
                column = (j - 2 * pair) * HD
                rows[pl.ds(place, 128, stride=24), :] = part[t * 128 : t * 128 + 128, column : column + HD]
    out[...] = rows[...].astype(BF16)


def qkv_partial(where, near, far, gain, weight):
    return call(
        qkv_body,
        shaped((128 * 24, HD), BF16),
        [SM, VM, VM, VM, HBM],
        [
            pltpu.VMEM((256, WIDTH), BF16),
            pltpu.VMEM((128 * 24, HD), F32),
            pltpu.VMEM((WIDTH, 1280), BF16),
            DMA,
        ],
    )(where, near, far, gain, hbm(weight))


def turn(vectors, cosine, sine):
    return vectors * cosine + pltpu.roll(vectors, HD // 2, vectors.ndim - 1) * sine


def attend_body(angles, received, keys, values, out, fresh, scores, held, sem):
    fetch = pltpu.make_async_copy(values, held, sem)
    fetch.start()
    total = received[0].astype(F32)
    for i in range(1, NX):
        total = total + received[i].astype(F32)
    squares = total[:, 20:24, :]
    scales = []
    for t in range(2):
        square = squares[:, 2 * t : 2 * t + 1, :] + squares[:, 2 * t + 1 : 2 * t + 2, :]
        scales.append(lax.rsqrt(square / D + EPSILON))
    cosines = [angles[2 * t : 2 * t + 1, :] for t in range(2)]
    sines = [angles[2 * t + 1 : 2 * t + 2, :] for t in range(2)]
    queries, new_keys, new_values = [], [], []
    for t in range(2):
        head = (total[:, 8 * t : 8 * t + 8, :] * scales[t]).astype(BF16).astype(F32)
        flat = turn(head.reshape(64, HD), cosines[t], sines[t])
        queries.append((flat * HD**-0.5).astype(BF16).astype(F32).reshape(8, 8, HD))
        key = (total[:, 16 + t : 17 + t, :] * scales[t]).astype(BF16).astype(F32).reshape(8, HD)
        new_keys.append(turn(key, cosines[t], sines[t]).astype(BF16))
        value = (total[:, 18 + t : 19 + t, :] * scales[t]).astype(BF16).reshape(8, HD)
        new_values.append(value)
        fresh[0, t, :, :HD] = new_keys[t]
        fresh[0, t, :, HD:] = value
    both = jnp.concatenate(queries, axis=1)
    both16 = both.astype(BF16)
    for g in range(KVH):
        scores[g * 16 : g * 16 + 16, :] = lax.dot_general(
            both16[g], keys[0, g], (((1,), (1,)), ((), ())), preferred_element_type=F32
        )
    extra = []
    step = lax.broadcasted_iota(jnp.int32, (KVH, 16, 1), 1) // GQ
    for t in range(2):
        dots = jnp.sum(both * new_keys[t].astype(F32).reshape(KVH, 1, HD), axis=2, keepdims=True)
        if t == 1:
            dots = jnp.where(step >= 1, dots, -3.0e38)
        extra.append(dots.reshape(128, 1))
    cached = scores[...]
    top = jnp.maximum(jnp.max(cached, axis=1, keepdims=True), jnp.maximum(extra[0], extra[1]))
    cached = jnp.exp(cached - top)
    extra = [jnp.exp(value - top) for value in extra]
    share = 1.0 / (jnp.sum(cached, axis=1, keepdims=True) + extra[0] + extra[1])
    probs = (cached * share).astype(BF16)
    extra = [(value * share).astype(BF16).astype(F32).reshape(KVH, 16, 1) for value in extra]
    fetch.wait()
    for g in range(KVH):
        mixed = jnp.dot(probs[g * 16 : g * 16 + 16, :], held[0, g], preferred_element_type=F32)
        for t in range(2):
            mixed = mixed + extra[t][g] * new_values[t][g : g + 1, :].astype(F32)
        mixed = mixed.astype(BF16)
        for i in range(NX):
            out[i, g] = mixed


def attend(angles, received, keys, values):
    return call(
        attend_body,
        (shaped((NX, KVH, 16, HD), BF16), shaped((1, 2, KVH, 2 * HD), BF16)),
        [VM, VM, VM, HBM],
        [pltpu.VMEM((KVH * 16, CACHE), F32), pltpu.VMEM((1, KVH, CACHE, HD), BF16), DMA],
    )(angles, received, keys, hbm(values))


def out_body(where, received, weight, keep, send, wide, lhs, held, sem):
    fetch = pltpu.make_async_copy(weight, held, sem)
    fetch.start()
    mine = where[1]
    wide[...] = received[...].astype(F32)
    for flag in range(2):
        for k in range(4):
            block = mine ^ (2 * k + flag)
            for t in range(2):
                place = flag * 128 + k * 32 + t * 16
                for h in range(GQ):
                    start = block * 256 + t * 8 + h
                    lhs[place : place + 16, h * HD : h * HD + HD] = wide[
                        pl.ds(start, 16, stride=16), :
                    ].astype(BF16)
    fetch.wait()
    send[...] = jnp.dot(lhs[128:, :], held[...], preferred_element_type=F32).astype(BF16)
    keep[...] = jnp.dot(lhs[:128, :], held[...], preferred_element_type=F32)


def out_partial(where, received, weight):
    return call(
        out_body,
        (shaped((128, WIDTH), F32), shaped((128, WIDTH), BF16)),
        [SM, VM, HBM],
        [
            pltpu.VMEM((128 * 16, HD), F32),
            pltpu.VMEM((256, KVH * HD), BF16),
            pltpu.VMEM((KVH * HD, WIDTH), BF16),
            DMA,
        ],
    )(where, received, hbm(weight))


def add_body(turned, whole, other, total, send):
    for k in range(4):
        rows, theirs = slice(k * 32, k * 32 + 32), slice((k ^ turned) * 32, (k ^ turned) * 32 + 32)
        part = whole[rows, :] + other[theirs, :].astype(F32)
        total[rows, :] = part
        send[rows, :] = part.astype(BF16)


def residual_body(residual, gain, whole, other, after, normed):
    for k in range(4):
        rows, theirs = slice(k * 32, k * 32 + 32), slice((k ^ 3) * 32, (k ^ 3) * 32 + 32)
        part = residual[rows, :] + whole[rows, :] + other[theirs, :].astype(F32)
        normed[rows, :] = (part * gain[...]).astype(BF16)
        if k == 0:
            after[...] = part


def add_attention(residual, gain, keep, send):
    halves = (shaped((128, WIDTH), F32), shaped((128, WIDTH), BF16))
    whole, sent = call(functools.partial(add_body, 0), halves, [VM] * 2)(keep, swap_gy(send, 1))
    whole, sent = call(functools.partial(add_body, 1), halves, [VM] * 2)(whole, swap_gy(sent, 2))
    after, near = call(
        residual_body, (shaped((32, WIDTH), F32), shaped((128, WIDTH), BF16)), [VM] * 4
    )(residual, gain, whole, swap_gy(sent, 6))
    return after, near, swap_gy(near, 1)


def split_body(keep, other, own, *sends):
    whole = keep[...] + other[...].astype(F32)
    own[...] = whole[:32]
    for k, send in enumerate(sends):
        send[...] = whole[32 * k + 32 : 32 * k + 64].astype(BF16)


def final_body(residual, own, one, two, three, out):
    out[...] = residual[...] + (own[...] + one[...].astype(F32) + two[...].astype(F32) + three[...].astype(F32))


def add_ffn(after, keep, send):
    own, *sends = call(
        split_body,
        (shaped((32, WIDTH), F32),) + (shaped((32, WIDTH), BF16),) * 3,
        [VM, VM],
    )(keep, swap_gy(send, 1))
    pieces = [swap_gy(piece, 2 * (k + 1)) for k, piece in enumerate(sends)]
    return call(final_body, shaped((32, WIDTH), F32), [VM] * 5)(after, own, *pieces)


def rows_body(own, one, two, three, gain, residual, scaled):
    for k, piece in enumerate((own, one, two, three)):
        rows = slice(k * 32, k * 32 + 32)
        residual[rows, :] = piece[...]
        scaled[rows, :] = (piece[...] * gain[...]).astype(BF16)


def gather_rows(own, gain):
    pieces = [own] + [swap_gy(own, 2 * k) for k in (1, 2, 3)]
    residual, near = call(
        rows_body, (shaped((128, WIDTH), F32), shaped((128, WIDTH), BF16)), [VM] * 5
    )(*pieces, gain)
    return residual, near, swap_gy(near, 1)


def two_parts(squares):
    high = squares.astype(BF16).astype(F32)
    first = lax.broadcasted_iota(jnp.int32, squares.shape, 1) < HD // 2
    return jnp.where(first, high, squares - high).astype(BF16)


def one_part(parts):
    wide = parts.astype(F32)
    return wide + pltpu.roll(wide, HD // 2, 1)


def swap_by_core(array, first, second):
    pairs = []
    for i in range(NX):
        for j in range(NY):
            pairs.append((i * NY + j, (i ^ (second if j & 1 else first)) * NY + j))
    return lax.ppermute(array, ("gx", "gy"), pairs)


def place_of(flow, core, chunk):
    turned = jnp.where(core == 0, chunk, ((chunk << 2) | (chunk >> 2)) & 15)
    if flow == 1:
        turned = (turned & 3) | ((turned & 4) << 1) | ((turned & 8) >> 1)
    return turned


def gate_body(send, where, near, far, gain, gate, up, *refs):
    outs, lhs = refs[:2], refs[2]
    core = where[1] & 1
    for f in range(2):
        for flag, source in enumerate((near, far)):
            for k in range(4):
                block = where[1] ^ (2 * k + flag)
                for t in range(2):
                    place = place_of(f, core, (2 * block + t) ^ where[0])
                    start = pl.multiple_of(place * 16, 16)
                    lhs[f, pl.ds(start, 16), :] = source[k * 32 + t * 16 : k * 32 + t * 16 + 16, :]
    rows = slice(128, 256) if send else slice(0, 128)
    plain = lhs[0, rows, :].astype(F32) / gain[...]
    squares = jnp.broadcast_to(jnp.sum(plain * plain, axis=1, keepdims=True), (128, HD))
    outs[0][:, 2 * HALF :] = two_parts(squares) if send else squares
    for f in range(2):
        for i, weight in enumerate((gate, up)):
            part = jnp.dot(lhs[f, rows, :], weight[:, f * HALF : f * HALF + HALF], preferred_element_type=F32)
            outs[f][:, i * HALF : i * HALF + HALF] = part.astype(outs[f].dtype)


def gate_partial(send, *args):
    return call(
        functools.partial(gate_body, send),
        tuple(shaped((128, width), BF16 if send else F32) for width in WIDTHS),
        [SM] + [VM] * 5,
        [pltpu.VMEM((2, 256, WIDTH), BF16)],
    )(*args)


def halve_body(*refs):
    ins, outs = refs[:4], refs[4:]
    for f in range(2):
        keep, other = ins[2 * f], ins[2 * f + 1]
        whole = keep[:, : 2 * HALF] + other[:, : 2 * HALF].astype(F32)
        outs[2 * f][:, : 2 * HALF] = whole[:64]
        outs[2 * f + 1][:, : 2 * HALF] = whole[64:].astype(BF16)
        if f == 0:
            squares = keep[:, 2 * HALF :] + one_part(other[:, 2 * HALF :])
            outs[0][:, 2 * HALF :] = squares[:64]
            outs[1][:, 2 * HALF :] = two_parts(squares[64:])


def quarter_body(*refs):
    ins, outs = refs[:4], refs[4:]
    start = 0
    for f in range(2):
        keep, other = ins[2 * f], ins[2 * f + 1]
        whole = keep[:, : 2 * HALF] + other[:, : 2 * HALF].astype(F32)
        for k, out in enumerate(outs):
            rows = slice(gray(k) * 16, gray(k) * 16 + 16)
            out[:, start : start + 2 * HALF] = whole[rows].astype(out.dtype)
        if f == 0:
            squares = keep[:, 2 * HALF :] + one_part(other[:, 2 * HALF :])
            for k, out in enumerate(outs):
                part = squares[gray(k) * 16 : gray(k) * 16 + 16]
                out[:, 4 * HALF :] = part if k == 0 else two_parts(part)
        start += 2 * HALF


def hidden_body(own, one, two, three, out):
    others = (one, two, three)
    squares = own[:, 4 * HALF :] + sum(one_part(other[:, 4 * HALF :]) for other in others)
    scale = lax.rsqrt(squares / D + EPSILON)[:, :1]
    for f in range(2):
        gate, up = (
            (own[:, columns] + sum(other[:, columns].astype(F32) for other in others)) * scale
            for columns in (slice(i * HALF, i * HALF + HALF) for i in (2 * f, 2 * f + 1))
        )
        out[:, f * HALF : f * HALF + HALF] = (gate / (1.0 + jnp.exp(-gate)) * up).astype(BF16)


def hidden_units(*args):
    sends = gate_partial(True, *args)
    moved = [swap_by_core(sends[0], 4, 1), swap_by_core(sends[1], 12, 3)]
    keeps = gate_partial(False, *args)
    halves = []
    for width in WIDTHS:
        halves += [shaped((64, width), F32), shaped((64, width), BF16)]
    parts = call(halve_body, tuple(halves), [VM] * 4)(keeps[0], moved[0], keeps[1], moved[1])
    moved = [swap_by_core(parts[1], 12, 3), swap_by_core(parts[3], 4, 1)]
    wide = 4 * HALF + HD
    own, *sends = call(
        quarter_body, (shaped((16, wide), F32),) + (shaped((16, wide), BF16),) * 3, [VM] * 4
    )(parts[0], moved[0], parts[2], moved[1])
    moved = [swap_by_core(part, k, 4 * k) for k, part in zip((1, 2, 3), sends)]
    return call(hidden_body, shaped((16, UNITS), BF16), [VM] * 4)(own, *moved)


def stack_body(*refs):
    *pieces, out = refs
    rows = pieces[0].shape[0]
    for k, piece in enumerate(pieces):
        out[k * rows : k * rows + rows, :] = piece[...]


def down_body(where, *refs):
    pieces, (weight, keep, send, lhs) = refs[:4], refs[4:]
    core = where[1] & 1
    for m in range(4):
        for k in range(4):
            step = jnp.where(core == 0, gray(m) * 4 + gray(k), gray(k) * 4 + gray(m))
            place = where[0] ^ step
            block = (place >> 1) ^ where[1]
            start = (block & 1) * 128 + (block >> 1) * 32 + (place & 1) * 16
            lhs[pl.ds(pl.multiple_of(start, 16), 16), :] = pieces[m][k * 16 : k * 16 + 16, :]
    send[...] = jnp.dot(lhs[128:, :], weight[...], preferred_element_type=F32).astype(BF16)
    keep[...] = jnp.dot(lhs[:128, :], weight[...], preferred_element_type=F32)


def down_partial(where, units, weight):
    pieces = [units] + [swap_by_core(units, k, 4 * k) for k in (1, 2, 3)]
    near = call(stack_body, shaped((64, UNITS), BF16), [VM] * 4)(*pieces)
    pieces = [near] + [swap_by_core(near, 4 * k, k) for k in (1, 2, 3)]
    return call(
        down_body,
        (shaped((128, WIDTH), F32), shaped((128, WIDTH), BF16)),
        [SM] + [VM] * 5,
        [pltpu.VMEM((256, UNITS), BF16)],
    )(where, *pieces, weight)


def rotations(positions):
    frequency = jnp.exp(jnp.arange(HD // 2, dtype=F32) * (-2.0 / HD) * jnp.log(THETA))
    rows = []
    for t in range(2):
        angles = (positions + t).astype(F32) * frequency
        cosine, sine = jnp.cos(angles), jnp.sin(angles)
        rows += [jnp.concatenate([cosine, cosine]), jnp.concatenate([-sine, sine])]
    return jnp.stack(rows)


def per_device(
    inputs,
    positions,
    attn_gain,
    ffn_gain,
    qkv_weight,
    out_weight,
    gate_weight,
    up_weight,
    down_weight,
    k_cache,
    v_cache,
):
    gx, gy = lax.axis_index("gx"), lax.axis_index("gy")
    where = jnp.stack([gray(gx >> 2) * 4 + gray(gx & 3), gy]).astype(jnp.int32)
    angles = rotations(positions)
    attn_gain, ffn_gain = attn_gain.reshape(1, WIDTH), ffn_gain.reshape(1, WIDTH)

    residual, near, far = gather_rows(inputs.reshape(32, WIDTH), attn_gain)
    partial = qkv_partial(where, near, far, attn_gain, qkv_weight).reshape(128, 24, HD)
    received = lax.all_to_all(partial, ("gx", "gy"), 0, 0, tiled=True).reshape(NX, NY, 24, HD)
    attended, new_kv = attend(angles, received, k_cache, v_cache)
    heads = lax.all_to_all(attended.reshape(128, 16, HD), ("gx", "gy"), 0, 0, tiled=True)
    keep, send = out_partial(where, heads.reshape(128 * 16, HD), out_weight)
    after_attn, near, far = add_attention(residual, ffn_gain, keep, send)

    units = hidden_units(where, near, far, ffn_gain, gate_weight, up_weight)
    outputs = add_ffn(after_attn, *down_partial(where, units, down_weight))
    return outputs.reshape(2, 16, WIDTH), new_kv


def solution(mesh):
    placed = (
        P(None, "gy", "gx"),
        P(("gx", "gy")),
        P("gx"),
        P("gx"),
        P("gx", "gy"),
        P("gy", "gx"),
        P("gx", "gy"),
        P("gx", "gy"),
        P("gy", "gx"),
        P(("gx", "gy"), None, None, None),
        P(("gx", "gy"), None, None, None),
    )
    return jax.shard_map(
        per_device,
        mesh=mesh,
        in_specs=placed,
        out_specs=(P(None, "gy", "gx"), P(("gx", "gy"), None, None, None)),
        check_vma=False,
    )
```

```python
import functools

import jax
import jax.numpy as jnp
from jax import lax
from jax.experimental import pallas as pl
from jax.experimental.pallas import tpu as pltpu
from jax.sharding import PartitionSpec as P

D = 8192
KVH = 8
HD = 128
CACHE = 1024
GQ = 8
EPSILON = 1e-05
THETA = 500000.0
NX = 16
NY = 8
WIDTH = 512
UNITS = 3584
HALF = UNITS // 2
WIDTHS = (2 * HALF + HD, 2 * HALF)
F32 = jnp.float32
BF16 = jnp.bfloat16
MIB = 1 << 20

VM = pl.BlockSpec(memory_space=pltpu.VMEM)
SM = pl.BlockSpec(memory_space=pltpu.SMEM)
HBM = pl.BlockSpec(memory_space=pltpu.HBM)
ANY = pl.BlockSpec(memory_space=pl.ANY)


def swap_gx(array, bits):
    return lax.ppermute(array, "gx", [(i, i ^ bits) for i in range(NX)])


def swap_gy(array, bits):
    return lax.ppermute(array, "gy", [(i, i ^ bits) for i in range(NY)])


def swap_by_core(array, first, second, axis="gx"):
    pairs = []
    for i in range(NX):
        for j in range(NY):
            bits = second if j & 1 else first
            pairs.append((i * NY + j, (i ^ bits) * NY + j if axis == "gx" else i * NY + (j ^ bits)))
    return lax.ppermute(array, ("gx", "gy"), pairs)


def gray(place):
    return ((place & 1) ^ (place >> 1)) * 2 + (place >> 1)


def call(body, outs, ins, scratch=(), limit=14, cost=0):
    cost = pl.CostEstimate(flops=0, bytes_accessed=cost, transcendentals=0) if cost else None
    return pl.pallas_call(
        body,
        out_shape=outs,
        in_specs=ins,
        out_specs=jax.tree.map(lambda _: VM, outs),
        scratch_shapes=list(scratch),
        compiler_params=pltpu.CompilerParams(vmem_limit_bytes=limit * MIB),
        cost_estimate=cost,
    )


def hbm(array):
    return pltpu.with_memory_space_constraint(array, pltpu.HBM)


def shaped(shape, dtype):
    return jax.ShapeDtypeStruct(shape, dtype)


def bring_body(count, *refs):
    ins, outs, sems = refs[:count], refs[-1 - count : -1], refs[-1]
    fetches = [pltpu.make_async_copy(a, b, sems.at[i]) for i, (a, b) in enumerate(zip(ins, outs))]
    for fetch in fetches:
        fetch.start()
    for fetch in fetches:
        fetch.wait()


def bring(arrays, after):
    size = sum(a.size * a.dtype.itemsize for a in arrays)
    outs = pl.pallas_call(
        functools.partial(bring_body, len(arrays)),
        out_shape=tuple(pltpu.VMEM(a.shape, a.dtype) for a in arrays),
        in_specs=[HBM] * len(arrays) + [ANY] * len(after),
        out_specs=(VM,) * len(arrays),
        scratch_shapes=[pltpu.SemaphoreType.DMA((len(arrays),))],
        compiler_params=pltpu.CompilerParams(vmem_limit_bytes=14 * MIB),
        cost_estimate=pl.CostEstimate(flops=0, bytes_accessed=2 * size, transcendentals=0),
    )(*(hbm(a) for a in arrays), *after)
    return [pltpu.with_memory_space_constraint(a, pltpu.VMEM) for a in outs]


def qkv_body(where, near, far, gain, held, out, lhs, rows):
    mine = where[1]
    for flag, source in enumerate((near, far)):
        for k in range(4):
            block = mine ^ (2 * k + flag)
            for t in range(2):
                start = pl.multiple_of(t * 128 + block * 16, 16)
                lhs[pl.ds(start, 16), :] = source[k * 32 + t * 16 : k * 32 + t * 16 + 16, :]
    plain = lhs[...].astype(F32) / gain[...]
    squares = jnp.sum(plain * plain, axis=1, keepdims=True)
    for t in range(2):
        whole = jnp.broadcast_to(squares[t * 128 : t * 128 + 128], (128, HD))
        high = whole.astype(BF16).astype(F32)
        rows[pl.ds(20 + 2 * t, 128, stride=24), :] = high
        rows[pl.ds(21 + 2 * t, 128, stride=24), :] = whole - high
    for pair in range(5):
        part = jnp.dot(lhs[...], held[:, pair * 256 : pair * 256 + 256], preferred_element_type=F32)
        for j in (2 * pair, 2 * pair + 1):
            for t in range(2):
                place = t * 8 + j if j < GQ else 16 + (j - GQ) * 2 + t
                column = (j - 2 * pair) * HD
                rows[pl.ds(place, 128, stride=24), :] = part[t * 128 : t * 128 + 128, column : column + HD]
    out[...] = rows[...].astype(BF16)


def qkv_partial(where, near, far, gain, weight):
    return call(
        qkv_body,
        shaped((128 * 24, HD), BF16),
        [SM, VM, VM, VM, VM],
        [pltpu.VMEM((256, WIDTH), BF16), pltpu.VMEM((128 * 24, HD), F32)],
    )(where, near, far, gain, weight)


def turn(vectors, cosine, sine):
    return vectors * cosine + pltpu.roll(vectors, HD // 2, vectors.ndim - 1) * sine


def attend_body(angles, received, keys, values, order, out, fresh, scores, held, sems):
    fetches = []
    for i, cache in enumerate((keys, values)):
        for g in range(0, KVH, 2):
            fetch = pltpu.make_async_copy(cache.at[0, pl.ds(g, 2)], held.at[i, pl.ds(g, 2)], sems.at[i, g // 2])
            fetch.start()
            fetches.append(fetch)
    total = received[0].astype(F32)
    for i in range(1, NX):
        total = total + received[i].astype(F32)
    squares = total[:, 20:24, :]
    scales = []
    for t in range(2):
        square = squares[:, 2 * t : 2 * t + 1, :] + squares[:, 2 * t + 1 : 2 * t + 2, :]
        scales.append(lax.rsqrt(square / D + EPSILON))
    cosines = [angles[2 * t : 2 * t + 1, :] for t in range(2)]
    sines = [angles[2 * t + 1 : 2 * t + 2, :] for t in range(2)]
    queries, new_keys, new_values = [], [], []
    for t in range(2):
        head = (total[:, 8 * t : 8 * t + 8, :] * scales[t]).astype(BF16).astype(F32)
        flat = turn(head.reshape(64, HD), cosines[t], sines[t])
        queries.append((flat * HD**-0.5).astype(BF16).astype(F32).reshape(8, 8, HD))
        key = (total[:, 16 + t : 17 + t, :] * scales[t]).astype(BF16).astype(F32).reshape(8, HD)
        new_keys.append(turn(key, cosines[t], sines[t]).astype(BF16))
        value = (total[:, 18 + t : 19 + t, :] * scales[t]).astype(BF16).reshape(8, HD)
        new_values.append(value)
        fresh[0, t, :, :HD] = new_keys[t]
        fresh[0, t, :, HD:] = value
    both = jnp.concatenate(queries, axis=1)
    both16 = both.astype(BF16)
    for g in range(KVH):
        if g % 2 == 0:
            fetches[g // 2].wait()
        scores[g * 16 : g * 16 + 16, :] = lax.dot_general(
            both16[g], held[0, g], (((1,), (1,)), ((), ())), preferred_element_type=F32
        )
    extra = []
    step = lax.broadcasted_iota(jnp.int32, (KVH, 16, 1), 1) // GQ
    for t in range(2):
        dots = jnp.sum(both * new_keys[t].astype(F32).reshape(KVH, 1, HD), axis=2, keepdims=True)
        if t == 1:
            dots = jnp.where(step >= 1, dots, -3.0e38)
        extra.append(dots.reshape(128, 1))
    cached = scores[...]
    top = jnp.maximum(jnp.max(cached, axis=1, keepdims=True), jnp.maximum(extra[0], extra[1]))
    cached = jnp.exp(cached - top)
    extra = [jnp.exp(value - top) for value in extra]
    share = 1.0 / (jnp.sum(cached, axis=1, keepdims=True) + extra[0] + extra[1])
    probs = (cached * share).astype(BF16)
    extra = [(value * share).astype(BF16).astype(F32).reshape(KVH, 16, 1) for value in extra]
    for g in range(KVH):
        if g % 2 == 0:
            fetches[4 + g // 2].wait()
        mixed = jnp.dot(probs[g * 16 : g * 16 + 16, :], held[1, g], preferred_element_type=F32)
        for t in range(2):
            mixed = mixed + extra[t][g] * new_values[t][g : g + 1, :].astype(F32)
        mixed = mixed.astype(BF16)
        for i in range(NX):
            out[i, g] = mixed


def attend(angles, received, keys, values, order):
    return call(
        attend_body,
        (shaped((NX, KVH, 16, HD), BF16), shaped((1, 2, KVH, 2 * HD), BF16)),
        [VM, VM, HBM, HBM, ANY],
        [
            pltpu.VMEM((KVH * 16, CACHE), F32),
            pltpu.VMEM((2, KVH, CACHE, HD), BF16),
            pltpu.SemaphoreType.DMA((2, KVH // 2)),
        ],
    )(angles, received, hbm(keys), hbm(values), order)


def out_body(where, received, weight, twin, total, send, wide, lhs):
    wide[...] = received[...].astype(F32)
    for other in range(2):
        core = (where[1] & 1) ^ other
        for t in range(2):
            for h in range(GQ):
                column = (other * GQ + h) * HD
                lhs[t * 64 : t * 64 + 64, column : column + HD] = wide[
                    pl.ds(core * 16 + t * 8 + h, 64, stride=32), :
                ].astype(BF16)
    half = GQ * HD
    part = jnp.dot(lhs[:, :half], weight[...], preferred_element_type=F32)
    part = part + jnp.dot(lhs[:, half:], twin[...], preferred_element_type=F32)
    total[...] = part
    send[...] = part.astype(BF16)


def out_partial(where, received, mine, twin):
    return call(
        out_body,
        (shaped((128, WIDTH), F32), shaped((128, WIDTH), BF16)),
        [SM, VM, VM, VM],
        [pltpu.VMEM((64 * 32, HD), F32), pltpu.VMEM((128, 2 * GQ * HD), BF16)],
    )(where, received, mine, twin)


def add_body(whole, one, two, three, mine):
    total = whole[...] + (one[...].astype(F32) + two[...].astype(F32) + three[...].astype(F32))
    mine[...] = total.astype(BF16)


def sum_over_x(whole, sent):
    others = [swap_gy(sent, 2 * k) for k in (1, 2, 3)]
    mine = call(add_body, shaped((128, WIDTH), BF16), [VM] * 4)(whole, *others)
    return mine, swap_gy(mine, 1)


def residual_body(where, residual, far, attn_gain, ffn_gain, mine, twin, after, normed, sums, attention):
    core = where[1] & 1
    sums[0] = jnp.where(core == 0, mine[...].astype(F32), twin[...].astype(F32))
    sums[1] = jnp.where(core == 0, twin[...].astype(F32), mine[...].astype(F32))
    for flag in range(2):
        for k in range(4):
            block = where[1] ^ (2 * k + flag)
            for t in range(2):
                start = pl.multiple_of(t * 64 + block * 8, 8)
                place = flag * 128 + k * 32 + t * 16
                for odd in range(2):
                    for q in range(4):
                        attention[q, pl.ds(place + odd, 8, stride=2), :] = sums[
                            odd, pl.ds(start, 8), q * 128 : q * 128 + 128
                        ]
    for q in range(4):
        columns = slice(q * 128, q * 128 + 128)
        first = residual[:, columns] + attention[q, :128, :]
        after[:, columns] = first[:32]
        normed[:128, columns] = (first * ffn_gain[:, columns]).astype(BF16)
        second = far[:, columns].astype(F32) / attn_gain[:, columns] + attention[q, 128:, :]
        normed[128:, columns] = (second * ffn_gain[:, columns]).astype(BF16)


def add_attention(where, residual, far, attn_gain, ffn_gain, sums):
    return call(
        residual_body,
        (shaped((32, WIDTH), F32), shaped((256, WIDTH), BF16)),
        [SM] + [VM] * 6,
        [pltpu.VMEM((2, 128, WIDTH), F32), pltpu.VMEM((4, 256, HD), F32)],
    )(where, residual, far, attn_gain, ffn_gain, *sums)


def split_body(keep, other, own, *sends):
    whole = keep[...] + other[...].astype(F32)
    own[...] = whole[:32]
    for k, send in enumerate(sends):
        send[...] = whole[32 * k + 32 : 32 * k + 64].astype(BF16)


def final_body(residual, own, one, two, three, out):
    out[...] = residual[...] + (own[...] + one[...].astype(F32) + two[...].astype(F32) + three[...].astype(F32))


def add_ffn(after, keep, send):
    own, *sends = call(
        split_body,
        (shaped((32, WIDTH), F32),) + (shaped((32, WIDTH), BF16),) * 3,
        [VM, VM],
    )(keep, swap_gy(send, 1))
    pieces = [swap_gy(piece, 2 * (k + 1)) for k, piece in enumerate(sends)]
    return call(final_body, shaped((32, WIDTH), F32), [VM] * 5)(after, own, *pieces)


def rows_body(own, one, two, three, gain, residual, scaled, held, sems):
    fetches = [
        pltpu.make_async_copy(gain, held, sems.at[0]),
        pltpu.make_async_copy(own, residual.at[pl.ds(0, 32)], sems.at[1]),
    ]
    for fetch in fetches:
        fetch.start()
    for k, piece in enumerate((one, two, three)):
        residual[k * 32 + 32 : k * 32 + 64, :] = piece[...]
    for fetch in fetches:
        fetch.wait()
    scaled[...] = (residual[...] * held[...]).astype(BF16)


def gather_rows(own, gain):
    pieces = [swap_gy(own, 2 * k) for k in (1, 2, 3)]
    residual, near, gain = call(
        rows_body,
        (shaped((128, WIDTH), F32), shaped((128, WIDTH), BF16), shaped((1, WIDTH), F32)),
        [HBM] + [VM] * 3 + [HBM],
        [pltpu.SemaphoreType.DMA((2,))],
    )(hbm(own), *pieces, hbm(gain))
    return residual, near, swap_gy(near, 1), gain


def two_parts(squares):
    high = squares.astype(BF16).astype(F32)
    first = lax.broadcasted_iota(jnp.int32, squares.shape, 1) < HD // 2
    return jnp.where(first, high, squares - high).astype(BF16)


def one_part(parts):
    wide = parts.astype(F32)
    return wide + pltpu.roll(wide, HD // 2, 1)


def place_of(flow, core, chunk):
    turned = jnp.where(core == 0, chunk, ((chunk << 2) | (chunk >> 2)) & 15)
    if flow == 1:
        turned = (turned & 3) | ((turned & 4) << 1) | ((turned & 8) >> 1)
    return turned


def gate_body(send, where, acts, gain, gate, up, *refs):
    outs, lhs = refs[:2], refs[2]
    core = where[1] & 1
    for f in range(2):
        for chunk in range(16):
            block = where[1] ^ (2 * ((chunk >> 1) & 3) + (chunk >> 3))
            place = place_of(f, core, (2 * block + (chunk & 1)) ^ where[0])
            start = pl.multiple_of(place * 16, 16)
            lhs[f, pl.ds(start, 16), :] = acts[chunk * 16 : chunk * 16 + 16, :]
    rows = slice(128, 256) if send else slice(0, 128)
    plain = lhs[0, rows, :].astype(F32) / gain[...]
    squares = jnp.broadcast_to(jnp.sum(plain * plain, axis=1, keepdims=True), (128, HD))
    outs[0][:, 2 * HALF :] = two_parts(squares) if send else squares
    for f in range(2):
        for i, weight in enumerate((gate, up)):
            part = jnp.dot(lhs[f, rows, :], weight[:, f * HALF : f * HALF + HALF], preferred_element_type=F32)
            outs[f][:, i * HALF : i * HALF + HALF] = part.astype(outs[f].dtype)


def gate_partial(send, *args):
    return call(
        functools.partial(gate_body, send),
        tuple(shaped((128, width), BF16 if send else F32) for width in WIDTHS),
        [SM] + [VM] * 4,
        [pltpu.VMEM((2, 256, WIDTH), BF16)],
    )(*args)


def halve_body(*refs):
    ins, outs = refs[:4], refs[4:]
    for f in range(2):
        keep, other = ins[2 * f], ins[2 * f + 1]
        whole = keep[:, : 2 * HALF] + other[:, : 2 * HALF].astype(F32)
        outs[2 * f][:, : 2 * HALF] = whole[:64]
        outs[2 * f + 1][:, : 2 * HALF] = whole[64:].astype(BF16)
        if f == 0:
            squares = keep[:, 2 * HALF :] + one_part(other[:, 2 * HALF :])
            outs[0][:, 2 * HALF :] = squares[:64]
            outs[1][:, 2 * HALF :] = two_parts(squares[64:])


def quarter_body(*refs):
    ins, outs = refs[:4], refs[4:]
    start = 0
    for f in range(2):
        keep, other = ins[2 * f], ins[2 * f + 1]
        whole = keep[:, : 2 * HALF] + other[:, : 2 * HALF].astype(F32)
        for k, out in enumerate(outs):
            rows = slice(gray(k) * 16, gray(k) * 16 + 16)
            out[:, start : start + 2 * HALF] = whole[rows].astype(out.dtype)
        if f == 0:
            squares = keep[:, 2 * HALF :] + one_part(other[:, 2 * HALF :])
            for k, out in enumerate(outs):
                part = squares[gray(k) * 16 : gray(k) * 16 + 16]
                out[:, 4 * HALF :] = part if k == 0 else two_parts(part)
        start += 2 * HALF


def hidden_body(own, one, two, three, out):
    others = (one, two, three)
    squares = own[:, 4 * HALF :] + sum(one_part(other[:, 4 * HALF :]) for other in others)
    scale = lax.rsqrt(squares / D + EPSILON)[:, :1]
    for f in range(2):
        gate, up = (
            (own[:, columns] + sum(other[:, columns].astype(F32) for other in others)) * scale
            for columns in (slice(i * HALF, i * HALF + HALF) for i in (2 * f, 2 * f + 1))
        )
        out[:, f * HALF : f * HALF + HALF] = (gate / (1.0 + jnp.exp(-gate)) * up).astype(BF16)


def hidden_units(*args):
    sends = gate_partial(True, *args)
    moved = [swap_by_core(sends[0], 4, 1), swap_by_core(sends[1], 12, 3)]
    keeps = gate_partial(False, *args)
    halves = []
    for width in WIDTHS:
        halves += [shaped((64, width), F32), shaped((64, width), BF16)]
    parts = call(halve_body, tuple(halves), [VM] * 4)(keeps[0], moved[0], keeps[1], moved[1])
    moved = [swap_by_core(parts[1], 12, 3), swap_by_core(parts[3], 4, 1)]
    wide = 4 * HALF + HD
    own, *sends = call(
        quarter_body, (shaped((16, wide), F32),) + (shaped((16, wide), BF16),) * 3, [VM] * 4
    )(parts[0], moved[0], parts[2], moved[1])
    moved = [swap_by_core(part, k, 4 * k) for k, part in zip((1, 2, 3), sends)]
    return call(hidden_body, shaped((16, UNITS), BF16), [VM] * 4)(own, *moved)


def stack_body(*refs):
    *pieces, out = refs
    rows = pieces[0].shape[0]
    for k, piece in enumerate(pieces):
        out[k * rows : k * rows + rows, :] = piece[...]


def down_body(where, *refs):
    pieces, (weight, keep, send, lhs) = refs[:4], refs[4:]
    core = where[1] & 1
    for m in range(4):
        for k in range(4):
            step = jnp.where(core == 0, gray(m) * 4 + gray(k), gray(k) * 4 + gray(m))
            place = where[0] ^ step
            block = (place >> 1) ^ where[1]
            start = (block & 1) * 128 + (block >> 1) * 32 + (place & 1) * 16
            lhs[pl.ds(pl.multiple_of(start, 16), 16), :] = pieces[m][k * 16 : k * 16 + 16, :]
    send[...] = jnp.dot(lhs[128:, :], weight[...], preferred_element_type=F32).astype(BF16)
    keep[...] = jnp.dot(lhs[:128, :], weight[...], preferred_element_type=F32)


def down_partial(where, units, weight):
    pieces = [units] + [swap_by_core(units, k, 4 * k) for k in (1, 2, 3)]
    near = call(stack_body, shaped((64, UNITS), BF16), [VM] * 4)(*pieces)
    pieces = [near] + [swap_by_core(near, 4 * k, k) for k in (1, 2, 3)]
    return call(
        down_body,
        (shaped((128, WIDTH), F32), shaped((128, WIDTH), BF16)),
        [SM] + [VM] * 5,
        [pltpu.VMEM((256, UNITS), BF16)],
    )(where, *pieces, weight)


def rotations(positions):
    frequency = jnp.exp(jnp.arange(HD // 2, dtype=F32) * (-2.0 / HD) * jnp.log(THETA))
    rows = []
    for t in range(2):
        angles = (positions + t).astype(F32) * frequency
        cosine, sine = jnp.cos(angles), jnp.sin(angles)
        rows += [jnp.concatenate([cosine, cosine]), jnp.concatenate([-sine, sine])]
    return jnp.stack(rows)


def per_device(
    inputs,
    positions,
    attn_gain,
    ffn_gain,
    qkv_weight,
    out_weight,
    gate_weight,
    up_weight,
    down_weight,
    k_cache,
    v_cache,
):
    gx, gy = lax.axis_index("gx"), lax.axis_index("gy")
    where = jnp.stack([gray(gx >> 2) * 4 + gray(gx & 3), gy]).astype(jnp.int32)
    angles = rotations(positions)
    attn_gain, ffn_gain = attn_gain.reshape(1, WIDTH), ffn_gain.reshape(1, WIDTH)

    twin = swap_gy(out_weight, 1)
    residual, near, far, attn_gain = gather_rows(inputs.reshape(32, WIDTH), attn_gain)
    (qkv_weight,) = bring((qkv_weight,), (near,))
    partial = qkv_partial(where, near, far, attn_gain, qkv_weight)
    out_weight, twin = bring((out_weight, twin), (partial,))
    partial = partial.reshape(128, 24, HD)
    received = lax.all_to_all(partial, ("gx", "gy"), 0, 0, tiled=True).reshape(NX, NY, 24, HD)
    attended, new_kv = attend(angles, received, k_cache, v_cache, out_weight)
    heads = lax.all_to_all(
        attended.reshape(64, 32, HD),
        ("gx", "gy"),
        0,
        0,
        axis_index_groups=[[i * NY + 2 * j + core for i in range(NX) for j in range(NY // 2)] for core in range(2)],
        tiled=True,
    )
    even_odd = sum_over_x(*out_partial(where, heads.reshape(64 * 32, HD), out_weight, twin))
    after_attn, normed = add_attention(where, residual, far, attn_gain, ffn_gain, even_odd)

    units = hidden_units(where, normed, ffn_gain, gate_weight, up_weight)
    outputs = add_ffn(after_attn, *down_partial(where, units, down_weight))
    return outputs.reshape(2, 16, WIDTH), new_kv


def solution(mesh):
    placed = (
        P(None, "gy", "gx"),
        P(("gx", "gy")),
        P("gx"),
        P("gx"),
        P("gx", "gy"),
        P("gy", "gx"),
        P("gx", "gy"),
        P("gx", "gy"),
        P("gy", "gx"),
        P(("gx", "gy"), None, None, None),
        P(("gx", "gy"), None, None, None),
    )
    return jax.shard_map(
        per_device,
        mesh=mesh,
        in_specs=placed,
        out_specs=(P(None, "gy", "gx"), P(("gx", "gy"), None, None, None)),
        check_vma=False,
    )
```

```python
import functools

import jax
import jax.numpy as jnp
from jax import lax
from jax.experimental import pallas as pl
from jax.experimental.pallas import tpu as pltpu
from jax.sharding import PartitionSpec as P

D = 8192
KVH = 8
HD = 128
CACHE = 1024
GQ = 8
EPSILON = 1e-05
THETA = 500000.0
NX = 16
NY = 8
WIDTH = 512
UNITS = 3584
HALF = UNITS // 2
WIDTHS = (2 * HALF + HD, 2 * HALF)
F32 = jnp.float32
BF16 = jnp.bfloat16
MIB = 1 << 20

VM = pl.BlockSpec(memory_space=pltpu.VMEM)
SM = pl.BlockSpec(memory_space=pltpu.SMEM)
HBM = pl.BlockSpec(memory_space=pltpu.HBM)
ANY = pl.BlockSpec(memory_space=pl.ANY)


def swap_gx(array, bits):
    return lax.ppermute(array, "gx", [(i, i ^ bits) for i in range(NX)])


def swap_gy(array, bits):
    return lax.ppermute(array, "gy", [(i, i ^ bits) for i in range(NY)])


def swap_by_core(array, first, second, axis="gx"):
    pairs = []
    for i in range(NX):
        for j in range(NY):
            bits = second if j & 1 else first
            pairs.append((i * NY + j, (i ^ bits) * NY + j if axis == "gx" else i * NY + (j ^ bits)))
    return lax.ppermute(array, ("gx", "gy"), pairs)


def gray(place):
    return ((place & 1) ^ (place >> 1)) * 2 + (place >> 1)


def call(body, outs, ins, scratch=(), limit=14, cost=0):
    cost = pl.CostEstimate(flops=0, bytes_accessed=cost, transcendentals=0) if cost else None
    return pl.pallas_call(
        body,
        out_shape=outs,
        in_specs=ins,
        out_specs=jax.tree.map(lambda _: VM, outs),
        scratch_shapes=list(scratch),
        compiler_params=pltpu.CompilerParams(vmem_limit_bytes=limit * MIB),
        cost_estimate=cost,
    )


def hbm(array):
    return pltpu.with_memory_space_constraint(array, pltpu.HBM)


def shaped(shape, dtype):
    return jax.ShapeDtypeStruct(shape, dtype)


def bring_body(count, *refs):
    ins, outs, sems = refs[:count], refs[-1 - count : -1], refs[-1]
    fetches = [pltpu.make_async_copy(a, b, sems.at[i]) for i, (a, b) in enumerate(zip(ins, outs))]
    for fetch in fetches:
        fetch.start()
    for fetch in fetches:
        fetch.wait()


def bring(arrays, after):
    size = sum(a.size * a.dtype.itemsize for a in arrays)
    outs = pl.pallas_call(
        functools.partial(bring_body, len(arrays)),
        out_shape=tuple(pltpu.VMEM(a.shape, a.dtype) for a in arrays),
        in_specs=[HBM] * len(arrays) + [ANY] * len(after),
        out_specs=(VM,) * len(arrays),
        scratch_shapes=[pltpu.SemaphoreType.DMA((len(arrays),))],
        compiler_params=pltpu.CompilerParams(vmem_limit_bytes=14 * MIB),
        cost_estimate=pl.CostEstimate(flops=0, bytes_accessed=2 * size, transcendentals=0),
    )(*(hbm(a) for a in arrays), *after)
    return [pltpu.with_memory_space_constraint(a, pltpu.VMEM) for a in outs]


def qkv_body(where, near, far, gain, held, out, lhs, rows):
    mine = where[1]
    for flag, source in enumerate((near, far)):
        for k in range(4):
            block = mine ^ (2 * k + flag)
            for t in range(2):
                start = pl.multiple_of(t * 128 + block * 16, 16)
                lhs[pl.ds(start, 16), :] = source[k * 32 + t * 16 : k * 32 + t * 16 + 16, :]
    plain = lhs[...].astype(F32) / gain[...]
    squares = jnp.sum(plain * plain, axis=1, keepdims=True)
    for t in range(2):
        whole = jnp.broadcast_to(squares[t * 128 : t * 128 + 128], (128, HD))
        high = whole.astype(BF16).astype(F32)
        rows[pl.ds(20 + 2 * t, 128, stride=24), :] = high
        rows[pl.ds(21 + 2 * t, 128, stride=24), :] = whole - high
    for pair in range(5):
        part = jnp.dot(lhs[...], held[:, pair * 256 : pair * 256 + 256], preferred_element_type=F32)
        for j in (2 * pair, 2 * pair + 1):
            for t in range(2):
                place = t * 8 + j if j < GQ else 16 + (j - GQ) * 2 + t
                column = (j - 2 * pair) * HD
                rows[pl.ds(place, 128, stride=24), :] = part[t * 128 : t * 128 + 128, column : column + HD]
    out[...] = rows[...].astype(BF16)


def qkv_partial(where, near, far, gain, weight):
    return call(
        qkv_body,
        shaped((128 * 24, HD), BF16),
        [SM, VM, VM, VM, VM],
        [pltpu.VMEM((256, WIDTH), BF16), pltpu.VMEM((128 * 24, HD), F32)],
    )(where, near, far, gain, weight)


def turn(vectors, cosine, sine):
    return vectors * cosine + pltpu.roll(vectors, HD // 2, vectors.ndim - 1) * sine


def attend_body(angles, received, keys, values, order, out, fresh, scores, held, sems):
    fetches = [pltpu.make_async_copy(a.at[0], held.at[i], sems.at[i]) for i, a in enumerate((keys, values))]
    for fetch in fetches:
        fetch.start()
    total = received[0].astype(F32)
    for i in range(1, NX):
        total = total + received[i].astype(F32)
    squares = total[:, 20:24, :]
    scales = []
    for t in range(2):
        square = squares[:, 2 * t : 2 * t + 1, :] + squares[:, 2 * t + 1 : 2 * t + 2, :]
        scales.append(lax.rsqrt(square / D + EPSILON))
    cosines = [angles[2 * t : 2 * t + 1, :] for t in range(2)]
    sines = [angles[2 * t + 1 : 2 * t + 2, :] for t in range(2)]
    queries, new_keys, new_values = [], [], []
    for t in range(2):
        head = (total[:, 8 * t : 8 * t + 8, :] * scales[t]).astype(BF16).astype(F32)
        flat = turn(head.reshape(64, HD), cosines[t], sines[t])
        queries.append((flat * HD**-0.5).astype(BF16).astype(F32).reshape(8, 8, HD))
        key = (total[:, 16 + t : 17 + t, :] * scales[t]).astype(BF16).astype(F32).reshape(8, HD)
        new_keys.append(turn(key, cosines[t], sines[t]).astype(BF16))
        value = (total[:, 18 + t : 19 + t, :] * scales[t]).astype(BF16).reshape(8, HD)
        new_values.append(value)
        fresh[0, t, :, :HD] = new_keys[t]
        fresh[0, t, :, HD:] = value
    both = jnp.concatenate(queries, axis=1)
    both16 = both.astype(BF16)
    fetches[0].wait()
    for g in range(KVH):
        scores[g * 16 : g * 16 + 16, :] = lax.dot_general(
            both16[g], held[0, g], (((1,), (1,)), ((), ())), preferred_element_type=F32
        )
    extra = []
    step = lax.broadcasted_iota(jnp.int32, (KVH, 16, 1), 1) // GQ
    for t in range(2):
        dots = jnp.sum(both * new_keys[t].astype(F32).reshape(KVH, 1, HD), axis=2, keepdims=True)
        if t == 1:
            dots = jnp.where(step >= 1, dots, -3.0e38)
        extra.append(dots.reshape(128, 1))
    cached = scores[...]
    top = jnp.maximum(jnp.max(cached, axis=1, keepdims=True), jnp.maximum(extra[0], extra[1]))
    cached = jnp.exp(cached - top)
    extra = [jnp.exp(value - top) for value in extra]
    share = 1.0 / (jnp.sum(cached, axis=1, keepdims=True) + extra[0] + extra[1])
    probs = (cached * share).astype(BF16)
    extra = [(value * share).astype(BF16).astype(F32).reshape(KVH, 16, 1) for value in extra]
    fetches[1].wait()
    for g in range(KVH):
        mixed = jnp.dot(probs[g * 16 : g * 16 + 16, :], held[1, g], preferred_element_type=F32)
        for t in range(2):
            mixed = mixed + extra[t][g] * new_values[t][g : g + 1, :].astype(F32)
        mixed = mixed.astype(BF16)
        for i in range(NX):
            out[i, g] = mixed


def attend(angles, received, keys, values, order):
    return call(
        attend_body,
        (shaped((NX, KVH, 16, HD), BF16), shaped((1, 2, KVH, 2 * HD), BF16)),
        [VM, VM, HBM, HBM, ANY],
        [
            pltpu.VMEM((KVH * 16, CACHE), F32),
            pltpu.VMEM((2, KVH, CACHE, HD), BF16),
            pltpu.SemaphoreType.DMA((2,)),
        ],
    )(angles, received, hbm(keys), hbm(values), order)


def out_body(where, received, weight, twin, total, send, wide, lhs):
    wide[...] = received[...].astype(F32)
    for other in range(2):
        core = (where[1] & 1) ^ other
        for t in range(2):
            for h in range(GQ):
                column = (other * GQ + h) * HD
                lhs[t * 64 : t * 64 + 64, column : column + HD] = wide[
                    pl.ds(core * 16 + t * 8 + h, 64, stride=32), :
                ].astype(BF16)
    half = GQ * HD
    part = jnp.dot(lhs[:, :half], weight[...], preferred_element_type=F32)
    part = part + jnp.dot(lhs[:, half:], twin[...], preferred_element_type=F32)
    total[...] = part
    send[...] = part.astype(BF16)


def out_partial(where, received, mine, twin):
    return call(
        out_body,
        (shaped((128, WIDTH), F32), shaped((128, WIDTH), BF16)),
        [SM, VM, VM, VM],
        [pltpu.VMEM((64 * 32, HD), F32), pltpu.VMEM((128, 2 * GQ * HD), BF16)],
    )(where, received, mine, twin)


def add_body(whole, three, one, two, mine):
    total = whole[...] + (one[...].astype(F32) + two[...].astype(F32) + three[...].astype(F32))
    mine[...] = total.astype(BF16)


def sum_over_x(whole, sent):
    others = [swap_gy(sent, 2 * k) for k in (3, 1, 2)]
    mine = call(add_body, shaped((128, WIDTH), BF16), [VM] * 4)(whole, *others)
    return mine, swap_gy(mine, 1)


def split_body(keep, other, own, *sends):
    whole = keep[...] + other[...].astype(F32)
    own[...] = whole[:32]
    for k, send in enumerate(sends):
        send[...] = whole[32 * k + 32 : 32 * k + 64].astype(BF16)


def final_body(residual, own, two, one, three, out):
    out[...] = residual[...] + (own[...] + one[...].astype(F32) + two[...].astype(F32) + three[...].astype(F32))


def add_ffn(after, keep, other):
    own, *sends = call(
        split_body,
        (shaped((32, WIDTH), F32),) + (shaped((32, WIDTH), BF16),) * 3,
        [VM, VM],
    )(keep, other)
    pieces = [swap_gy(sends[k - 1], 2 * k) for k in (2, 1, 3)]
    return call(final_body, shaped((32, WIDTH), F32), [VM] * 5)(after, own, *pieces)


def rows_body(own, one, two, three, gain, residual, scaled):
    for k, piece in enumerate((own, one, two, three)):
        rows = slice(k * 32, k * 32 + 32)
        residual[rows, :] = piece[...]
        scaled[rows, :] = (piece[...] * gain[...]).astype(BF16)


def gather_rows(own, gain):
    pieces = [swap_gy(own, 2 * k) for k in (1, 2, 3)]
    own, gain = bring((own, gain), ())
    residual, near = call(
        rows_body, (shaped((128, WIDTH), F32), shaped((128, WIDTH), BF16)), [VM] * 5
    )(own, *pieces, gain)
    return residual, near, swap_gy(near, 1), gain


def two_parts(squares):
    high = squares.astype(BF16).astype(F32)
    first = lax.broadcasted_iota(jnp.int32, squares.shape, 1) < HD // 2
    return jnp.where(first, high, squares - high).astype(BF16)


def one_part(parts):
    wide = parts.astype(F32)
    return wide + pltpu.roll(wide, HD // 2, 1)


def place_of(flow, core, chunk):
    turned = jnp.where(core == 0, chunk, ((chunk << 2) | (chunk >> 2)) & 15)
    if flow == 1:
        turned = (turned & 3) | ((turned & 4) << 1) | ((turned & 8) >> 1)
    return turned


def products(send, lhs, gain, gate, up, outs):
    rows = slice(128, 256) if send else slice(0, 128)
    plain = lhs[0, rows, :].astype(F32) / gain[...]
    squares = jnp.broadcast_to(jnp.sum(plain * plain, axis=1, keepdims=True), (128, HD))
    outs[0][:, 2 * HALF :] = two_parts(squares) if send else squares
    for f in range(2):
        for i, weight in enumerate((gate, up)):
            part = jnp.dot(lhs[f, rows, :], weight[:, f * HALF : f * HALF + HALF], preferred_element_type=F32)
            outs[f][:, i * HALF : i * HALF + HALF] = part.astype(outs[f].dtype)


def send_body(where, residual, far, attn_gain, gain, mine, twin, gate, up, after, lhs, first, second, sums, attention):
    core = where[1] & 1
    sums[0] = jnp.where(core == 0, mine[...].astype(F32), twin[...].astype(F32))
    sums[1] = jnp.where(core == 0, twin[...].astype(F32), mine[...].astype(F32))
    for chunk in range(16):
        block = where[1] ^ (2 * ((chunk >> 1) & 3) + (chunk >> 3))
        start = pl.multiple_of((chunk & 1) * 64 + block * 8, 8)
        for odd in range(2):
            for q in range(4):
                attention[q, pl.ds(chunk * 16 + odd, 8, stride=2), :] = sums[
                    odd, pl.ds(start, 8), q * 128 : q * 128 + 128
                ]
    for chunk in range(16):
        rows = slice(chunk * 16, chunk * 16 + 16)
        if chunk < 8:
            whole = residual[rows, :]
        else:
            whole = far[chunk * 16 - 128 : chunk * 16 - 112, :].astype(F32) / attn_gain[...]
        whole = whole + jnp.concatenate([attention[q, rows, :] for q in range(4)], axis=1)
        if chunk < 2:
            after[rows, :] = whole
        normed = (whole * gain[...]).astype(BF16)
        block = where[1] ^ (2 * ((chunk >> 1) & 3) + (chunk >> 3))
        for f in range(2):
            place = place_of(f, core, (2 * block + (chunk & 1)) ^ where[0])
            lhs[f, pl.ds(pl.multiple_of(place * 16, 16), 16), :] = normed
    products(True, lhs, gain, gate, up, (first, second))


def keep_body(lhs, gain, gate, up, first, second):
    products(False, lhs, gain, gate, up, (first, second))


def send_partial(where, residual, far, attn_gain, gain, sums, gate, up):
    return call(
        send_body,
        (shaped((32, WIDTH), F32), shaped((2, 256, WIDTH), BF16))
        + tuple(shaped((128, width), BF16) for width in WIDTHS),
        [SM] + [VM] * 8,
        [pltpu.VMEM((2, 128, WIDTH), F32), pltpu.VMEM((4, 256, HD), F32)],
    )(where, residual, far, attn_gain, gain, *sums, gate, up)


def halve_body(*refs):
    ins, outs = refs[:4], refs[4:]
    for f in range(2):
        keep, other = ins[2 * f], ins[2 * f + 1]
        whole = keep[:, : 2 * HALF] + other[:, : 2 * HALF].astype(F32)
        outs[2 * f][:, : 2 * HALF] = whole[:64]
        outs[2 * f + 1][:, : 2 * HALF] = whole[64:].astype(BF16)
        if f == 0:
            squares = keep[:, 2 * HALF :] + one_part(other[:, 2 * HALF :])
            outs[0][:, 2 * HALF :] = squares[:64]
            outs[1][:, 2 * HALF :] = two_parts(squares[64:])


def quarter_body(*refs):
    ins, outs = refs[:4], refs[4:]
    start = 0
    for f in range(2):
        keep, other = ins[2 * f], ins[2 * f + 1]
        whole = keep[:, : 2 * HALF] + other[:, : 2 * HALF].astype(F32)
        for k, out in enumerate(outs):
            rows = slice(gray(k) * 16, gray(k) * 16 + 16)
            out[:, start : start + 2 * HALF] = whole[rows].astype(out.dtype)
        if f == 0:
            squares = keep[:, 2 * HALF :] + one_part(other[:, 2 * HALF :])
            for k, out in enumerate(outs):
                part = squares[gray(k) * 16 : gray(k) * 16 + 16]
                out[:, 4 * HALF :] = part if k == 0 else two_parts(part)
        start += 2 * HALF


def hidden_body(own, one, three, two, out):
    others = (one, two, three)
    squares = own[:, 4 * HALF :] + sum(one_part(other[:, 4 * HALF :]) for other in others)
    scale = lax.rsqrt(squares / D + EPSILON)[:, :1]
    for f in range(2):
        gate, up = (
            (own[:, columns] + sum(other[:, columns].astype(F32) for other in others)) * scale
            for columns in (slice(i * HALF, i * HALF + HALF) for i in (2 * f, 2 * f + 1))
        )
        out[:, f * HALF : f * HALF + HALF] = (gate / (1.0 + jnp.exp(-gate)) * up).astype(BF16)


def hidden_units(lhs, gain, gate, up, sends):
    moved = [swap_by_core(sends[0], 4, 1), swap_by_core(sends[1], 12, 3)]
    keeps = call(keep_body, tuple(shaped((128, width), F32) for width in WIDTHS), [VM] * 4)(lhs, gain, gate, up)
    halves = []
    for width in WIDTHS:
        halves += [shaped((64, width), F32), shaped((64, width), BF16)]
    parts = call(halve_body, tuple(halves), [VM] * 4)(keeps[0], moved[0], keeps[1], moved[1])
    moved = [swap_by_core(parts[1], 12, 3), swap_by_core(parts[3], 4, 1)]
    wide = 4 * HALF + HD
    own, *sends = call(
        quarter_body, (shaped((16, wide), F32),) + (shaped((16, wide), BF16),) * 3, [VM] * 4
    )(parts[0], moved[0], parts[2], moved[1])
    moved = [swap_by_core(sends[k - 1], k, 4 * k) for k in (1, 3, 2)]
    return call(hidden_body, shaped((16, UNITS), BF16), [VM] * 4)(own, *moved)


def stack_body(*refs):
    *pieces, out = refs
    rows = pieces[0].shape[0]
    for k, piece in enumerate(pieces):
        out[k * rows : k * rows + rows, :] = piece[...]


def down_body(where, *refs):
    pieces, (weight, send, lhs) = refs[:4], refs[4:]
    core = where[1] & 1
    for m in range(4):
        for k in range(4):
            step = jnp.where(core == 0, gray(m) * 4 + gray(k), gray(k) * 4 + gray(m))
            place = where[0] ^ step
            block = (place >> 1) ^ where[1]
            start = (block & 1) * 128 + (block >> 1) * 32 + (place & 1) * 16
            lhs[pl.ds(pl.multiple_of(start, 16), 16), :] = pieces[m][k * 16 : k * 16 + 16, :]
    send[...] = jnp.dot(lhs[128:, :], weight[...], preferred_element_type=F32).astype(BF16)


def own_body(lhs, weight, keep):
    keep[...] = jnp.dot(lhs[:128, :], weight[...], preferred_element_type=F32)


def down_partial(where, units, weight):
    pieces = [units] + [swap_by_core(units, k, 4 * k) for k in (1, 2, 3)]
    near = call(stack_body, shaped((64, UNITS), BF16), [VM] * 4)(*pieces)
    pieces = [near] + [swap_by_core(near, 4 * k, k) for k in (1, 2, 3)]
    send, lhs = call(
        down_body, (shaped((128, WIDTH), BF16), shaped((256, UNITS), BF16)), [SM] + [VM] * 5
    )(where, *pieces, weight)
    other = swap_gy(send, 1)
    return call(own_body, shaped((128, WIDTH), F32), [VM] * 2)(lhs, weight), other


def rotations(positions):
    frequency = jnp.exp(jnp.arange(HD // 2, dtype=F32) * (-2.0 / HD) * jnp.log(THETA))
    rows = []
    for t in range(2):
        angles = (positions + t).astype(F32) * frequency
        cosine, sine = jnp.cos(angles), jnp.sin(angles)
        rows += [jnp.concatenate([cosine, cosine]), jnp.concatenate([-sine, sine])]
    return jnp.stack(rows)


def per_device(
    inputs,
    positions,
    attn_gain,
    ffn_gain,
    qkv_weight,
    out_weight,
    gate_weight,
    up_weight,
    down_weight,
    k_cache,
    v_cache,
):
    gx, gy = lax.axis_index("gx"), lax.axis_index("gy")
    where = jnp.stack([gray(gx >> 2) * 4 + gray(gx & 3), gy]).astype(jnp.int32)
    angles = rotations(positions)
    attn_gain, ffn_gain = attn_gain.reshape(1, WIDTH), ffn_gain.reshape(1, WIDTH)

    twin = swap_gy(out_weight, 1)
    residual, near, far, attn_gain = gather_rows(inputs.reshape(32, WIDTH), attn_gain)
    (qkv_weight,) = bring((qkv_weight,), (near,))
    partial = qkv_partial(where, near, far, attn_gain, qkv_weight)
    out_weight, twin = bring((out_weight, twin), (partial,))
    partial = partial.reshape(128, 24, HD)
    received = lax.all_to_all(partial, ("gx", "gy"), 0, 0, tiled=True).reshape(NX, NY, 24, HD)
    attended, new_kv = attend(angles, received, k_cache, v_cache, out_weight)
    heads = lax.all_to_all(
        attended.reshape(64, 32, HD),
        ("gx", "gy"),
        0,
        0,
        axis_index_groups=[[i * NY + 2 * j + core for i in range(NX) for j in range(NY // 2)] for core in range(2)],
        tiled=True,
    )
    even_odd = sum_over_x(*out_partial(where, heads.reshape(64 * 32, HD), out_weight, twin))
    after_attn, lhs, *sends = send_partial(
        where, residual, far, attn_gain, ffn_gain, even_odd, gate_weight, up_weight
    )
    units = hidden_units(lhs, ffn_gain, gate_weight, up_weight, sends)
    outputs = add_ffn(after_attn, *down_partial(where, units, down_weight))
    return outputs.reshape(2, 16, WIDTH), new_kv


def solution(mesh):
    placed = (
        P(None, "gy", "gx"),
        P(("gx", "gy")),
        P("gx"),
        P("gx"),
        P("gx", "gy"),
        P("gy", "gx"),
        P("gx", "gy"),
        P("gx", "gy"),
        P("gy", "gx"),
        P(("gx", "gy"), None, None, None),
        P(("gx", "gy"), None, None, None),
    )
    return jax.shard_map(
        per_device,
        mesh=mesh,
        in_specs=placed,
        out_specs=(P(None, "gy", "gx"), P(("gx", "gy"), None, None, None)),
        check_vma=False,
    )
```

```python
import functools

import jax
import jax.numpy as jnp
from jax import lax
from jax.experimental import pallas as pl
from jax.experimental.pallas import tpu as pltpu
from jax.sharding import PartitionSpec as P

D = 8192
KVH = 8
HD = 128
CACHE = 1024
GQ = 8
EPSILON = 1e-05
THETA = 500000.0
NX = 16
NY = 8
WIDTH = 512
UNITS = 3584
HALF = UNITS // 2
WIDTHS = (2 * HALF + HD, 2 * HALF)
F32 = jnp.float32
BF16 = jnp.bfloat16
MIB = 1 << 20

VM = pl.BlockSpec(memory_space=pltpu.VMEM)
SM = pl.BlockSpec(memory_space=pltpu.SMEM)
HBM = pl.BlockSpec(memory_space=pltpu.HBM)
ANY = pl.BlockSpec(memory_space=pl.ANY)


def swap_gx(array, bits):
    return lax.ppermute(array, "gx", [(i, i ^ bits) for i in range(NX)])


def swap_gy(array, bits):
    return lax.ppermute(array, "gy", [(i, i ^ bits) for i in range(NY)])


def swap_by_core(array, first, second, axis="gx"):
    pairs = []
    for i in range(NX):
        for j in range(NY):
            bits = second if j & 1 else first
            pairs.append((i * NY + j, (i ^ bits) * NY + j if axis == "gx" else i * NY + (j ^ bits)))
    return lax.ppermute(array, ("gx", "gy"), pairs)


def gray(place):
    return ((place & 1) ^ (place >> 1)) * 2 + (place >> 1)


def call(body, outs, ins, scratch=(), limit=14, cost=0):
    cost = pl.CostEstimate(flops=0, bytes_accessed=cost, transcendentals=0) if cost else None
    return pl.pallas_call(
        body,
        out_shape=outs,
        in_specs=ins,
        out_specs=jax.tree.map(lambda _: VM, outs),
        scratch_shapes=list(scratch),
        compiler_params=pltpu.CompilerParams(vmem_limit_bytes=limit * MIB),
        cost_estimate=cost,
    )


def hbm(array):
    return pltpu.with_memory_space_constraint(array, pltpu.HBM)


def shaped(shape, dtype):
    return jax.ShapeDtypeStruct(shape, dtype)


def bring_body(count, *refs):
    ins, outs, sems = refs[:count], refs[count:-1], refs[-1]
    fetches = [pltpu.make_async_copy(a, b, sems.at[i]) for i, (a, b) in enumerate(zip(ins, outs))]
    for fetch in fetches:
        fetch.start()
    for fetch in fetches:
        fetch.wait()


def bring(arrays):
    size = sum(a.size * a.dtype.itemsize for a in arrays)
    outs = pl.pallas_call(
        functools.partial(bring_body, len(arrays)),
        out_shape=tuple(pltpu.VMEM(a.shape, a.dtype) for a in arrays),
        in_specs=[HBM] * len(arrays),
        out_specs=(VM,) * len(arrays),
        scratch_shapes=[pltpu.SemaphoreType.DMA((len(arrays),))],
        compiler_params=pltpu.CompilerParams(vmem_limit_bytes=14 * MIB),
        cost_estimate=pl.CostEstimate(flops=0, bytes_accessed=2 * size, transcendentals=0),
    )(*(hbm(a) for a in arrays))
    return [pltpu.with_memory_space_constraint(a, pltpu.VMEM) for a in outs]


def qkv_body(where, near, far, gain, held, angles, twin, out, lhs, rows):
    mine = where[1]
    for flag, source in enumerate((near, far)):
        for k in range(4):
            block = mine ^ (2 * k + flag)
            for t in range(2):
                start = pl.multiple_of(t * 128 + block * 16, 16)
                lhs[pl.ds(start, 16), :] = source[k * 32 + t * 16 : k * 32 + t * 16 + 16, :]
    plain = lhs[...].astype(F32) / gain[...]
    squares = jnp.sum(plain * plain, axis=1, keepdims=True)
    for t in range(2):
        whole = jnp.broadcast_to(squares[t * 128 : t * 128 + 128], (128, HD))
        high = whole.astype(BF16).astype(F32)
        rows[pl.ds(20 + 2 * t, 128, stride=24), :] = high
        rows[pl.ds(21 + 2 * t, 128, stride=24), :] = whole - high
    for pair in range(5):
        part = jnp.dot(lhs[...], held[:, pair * 256 : pair * 256 + 256], preferred_element_type=F32)
        for j in (2 * pair, 2 * pair + 1):
            for t in range(2):
                place = t * 8 + j if j < GQ else 16 + (j - GQ) * 2 + t
                column = (j - 2 * pair) * HD
                rows[pl.ds(place, 128, stride=24), :] = part[t * 128 : t * 128 + 128, column : column + HD]
    out[...] = rows[...].astype(BF16)


def qkv_partial(where, near, far, gain, weight, *order):
    return call(
        qkv_body,
        shaped((128 * 24, HD), BF16),
        [SM, VM, VM, VM, VM, ANY, ANY],
        [pltpu.VMEM((256, WIDTH), BF16), pltpu.VMEM((128 * 24, HD), F32)],
    )(where, near, far, gain, weight, *order)


def turn(vectors, cosine, sine):
    return vectors * cosine + pltpu.roll(vectors, HD // 2, vectors.ndim - 1) * sine


def attend_body(angles, received, keys, values, out, fresh, scores):
    total = received[0].astype(F32)
    for i in range(1, NX):
        total = total + received[i].astype(F32)
    squares = total[:, 20:24, :]
    scales = []
    for t in range(2):
        square = squares[:, 2 * t : 2 * t + 1, :] + squares[:, 2 * t + 1 : 2 * t + 2, :]
        scales.append(lax.rsqrt(square / D + EPSILON))
    cosines = [angles[2 * t : 2 * t + 1, :] for t in range(2)]
    sines = [angles[2 * t + 1 : 2 * t + 2, :] for t in range(2)]
    queries, new_keys, new_values = [], [], []
    for t in range(2):
        head = (total[:, 8 * t : 8 * t + 8, :] * scales[t]).astype(BF16).astype(F32)
        flat = turn(head.reshape(64, HD), cosines[t], sines[t])
        queries.append((flat * HD**-0.5).astype(BF16).astype(F32).reshape(8, 8, HD))
        key = (total[:, 16 + t : 17 + t, :] * scales[t]).astype(BF16).astype(F32).reshape(8, HD)
        new_keys.append(turn(key, cosines[t], sines[t]).astype(BF16))
        value = (total[:, 18 + t : 19 + t, :] * scales[t]).astype(BF16).reshape(8, HD)
        new_values.append(value)
        fresh[0, t, :, :HD] = new_keys[t]
        fresh[0, t, :, HD:] = value
    both = jnp.concatenate(queries, axis=1)
    both16 = both.astype(BF16)
    for g in range(KVH):
        scores[g * 16 : g * 16 + 16, :] = lax.dot_general(
            both16[g], keys[0, g], (((1,), (1,)), ((), ())), preferred_element_type=F32
        )
    extra = []
    step = lax.broadcasted_iota(jnp.int32, (KVH, 16, 1), 1) // GQ
    for t in range(2):
        dots = jnp.sum(both * new_keys[t].astype(F32).reshape(KVH, 1, HD), axis=2, keepdims=True)
        if t == 1:
            dots = jnp.where(step >= 1, dots, -3.0e38)
        extra.append(dots.reshape(128, 1))
    cached = scores[...]
    top = jnp.maximum(jnp.max(cached, axis=1, keepdims=True), jnp.maximum(extra[0], extra[1]))
    cached = jnp.exp(cached - top)
    extra = [jnp.exp(value - top) for value in extra]
    share = 1.0 / (jnp.sum(cached, axis=1, keepdims=True) + extra[0] + extra[1])
    probs = (cached * share).astype(BF16)
    extra = [(value * share).astype(BF16).astype(F32).reshape(KVH, 16, 1) for value in extra]
    for g in range(KVH):
        mixed = jnp.dot(probs[g * 16 : g * 16 + 16, :], values[0, g], preferred_element_type=F32)
        for t in range(2):
            mixed = mixed + extra[t][g] * new_values[t][g : g + 1, :].astype(F32)
        mixed = mixed.astype(BF16)
        for i in range(NX):
            out[i, g] = mixed


def attend(angles, received, keys, values):
    return call(
        attend_body,
        (shaped((NX, KVH, 16, HD), BF16), shaped((1, 2, KVH, 2 * HD), BF16)),
        [VM, VM, VM, VM],
        [pltpu.VMEM((KVH * 16, CACHE), F32)],
    )(angles, received, keys, values)


def out_body(where, received, weight, twin, total, send, wide, lhs):
    wide[...] = received[...].astype(F32)
    for other in range(2):
        core = (where[1] & 1) ^ other
        for t in range(2):
            for h in range(GQ):
                column = (other * GQ + h) * HD
                lhs[t * 64 : t * 64 + 64, column : column + HD] = wide[
                    pl.ds(core * 16 + t * 8 + h, 64, stride=32), :
                ].astype(BF16)
    half = GQ * HD
    part = jnp.dot(lhs[:, :half], weight[...], preferred_element_type=F32)
    part = part + jnp.dot(lhs[:, half:], twin[...], preferred_element_type=F32)
    total[...] = part
    send[...] = part.astype(BF16)


def out_partial(where, received, mine, twin):
    return call(
        out_body,
        (shaped((128, WIDTH), F32), shaped((128, WIDTH), BF16)),
        [SM, VM, VM, VM],
        [pltpu.VMEM((64 * 32, HD), F32), pltpu.VMEM((128, 2 * GQ * HD), BF16)],
    )(where, received, mine, twin)


def add_body(whole, three, one, two, mine):
    total = whole[...] + (one[...].astype(F32) + two[...].astype(F32) + three[...].astype(F32))
    mine[...] = total.astype(BF16)


def sum_over_x(whole, sent):
    others = [swap_gy(sent, 2 * k) for k in (3, 1, 2)]
    mine = call(add_body, shaped((128, WIDTH), BF16), [VM] * 4)(whole, *others)
    return mine, swap_gy(mine, 1)


def split_body(keep, other, own, *sends):
    whole = keep[...] + other[...].astype(F32)
    own[...] = whole[:32]
    for k, send in enumerate(sends):
        send[...] = whole[32 * k + 32 : 32 * k + 64].astype(BF16)


def final_body(residual, own, two, one, three, out):
    out[...] = residual[...] + (own[...] + one[...].astype(F32) + two[...].astype(F32) + three[...].astype(F32))


def add_ffn(after, keep, other):
    own, *sends = call(
        split_body,
        (shaped((32, WIDTH), F32),) + (shaped((32, WIDTH), BF16),) * 3,
        [VM, VM],
    )(keep, other)
    pieces = [swap_gy(sends[k - 1], 2 * k) for k in (2, 1, 3)]
    return call(final_body, shaped((32, WIDTH), F32), [VM] * 5)(after, own, *pieces)


def rows_body(own, one, two, three, gain, residual, scaled):
    for k, piece in enumerate((own, one, two, three)):
        rows = slice(k * 32, k * 32 + 32)
        residual[rows, :] = piece[...]
        scaled[rows, :] = (piece[...] * gain[...]).astype(BF16)


def gather_rows(own, gain, *weights):
    pieces = [swap_gy(own, 2 * k) for k in (1, 2, 3)]
    own, gain, *weights = bring((own, gain, *weights))
    residual, near = call(
        rows_body, (shaped((128, WIDTH), F32), shaped((128, WIDTH), BF16)), [VM] * 5
    )(own, *pieces, gain)
    return residual, near, swap_gy(near, 1), gain, *weights


def two_parts(squares):
    high = squares.astype(BF16).astype(F32)
    first = lax.broadcasted_iota(jnp.int32, squares.shape, 1) < HD // 2
    return jnp.where(first, high, squares - high).astype(BF16)


def one_part(parts):
    wide = parts.astype(F32)
    return wide + pltpu.roll(wide, HD // 2, 1)


def place_of(flow, core, chunk):
    turned = jnp.where(core == 0, chunk, ((chunk << 2) | (chunk >> 2)) & 15)
    if flow == 1:
        turned = (turned & 3) | ((turned & 4) << 1) | ((turned & 8) >> 1)
    return turned


def products(send, lhs, gain, gate, up, outs):
    rows = slice(128, 256) if send else slice(0, 128)
    plain = lhs[0, rows, :].astype(F32) / gain[...]
    squares = jnp.broadcast_to(jnp.sum(plain * plain, axis=1, keepdims=True), (128, HD))
    outs[0][:, 2 * HALF :] = two_parts(squares) if send else squares
    for f in range(2):
        for i, weight in enumerate((gate, up)):
            part = jnp.dot(lhs[f, rows, :], weight[:, f * HALF : f * HALF + HALF], preferred_element_type=F32)
            outs[f][:, i * HALF : i * HALF + HALF] = part.astype(outs[f].dtype)


def send_body(where, residual, far, attn_gain, gain, mine, twin, gate, up, after, lhs, first, second, sums, attention):
    core = where[1] & 1
    sums[0] = jnp.where(core == 0, mine[...].astype(F32), twin[...].astype(F32))
    sums[1] = jnp.where(core == 0, twin[...].astype(F32), mine[...].astype(F32))
    for chunk in range(16):
        block = where[1] ^ (2 * ((chunk >> 1) & 3) + (chunk >> 3))
        start = pl.multiple_of((chunk & 1) * 64 + block * 8, 8)
        for odd in range(2):
            for q in range(4):
                attention[q, pl.ds(chunk * 16 + odd, 8, stride=2), :] = sums[
                    odd, pl.ds(start, 8), q * 128 : q * 128 + 128
                ]
    for chunk in range(16):
        rows = slice(chunk * 16, chunk * 16 + 16)
        if chunk < 8:
            whole = residual[rows, :]
        else:
            whole = far[chunk * 16 - 128 : chunk * 16 - 112, :].astype(F32) / attn_gain[...]
        whole = whole + jnp.concatenate([attention[q, rows, :] for q in range(4)], axis=1)
        if chunk < 2:
            after[rows, :] = whole
        normed = (whole * gain[...]).astype(BF16)
        block = where[1] ^ (2 * ((chunk >> 1) & 3) + (chunk >> 3))
        for f in range(2):
            place = place_of(f, core, (2 * block + (chunk & 1)) ^ where[0])
            lhs[f, pl.ds(pl.multiple_of(place * 16, 16), 16), :] = normed
    products(True, lhs, gain, gate, up, (first, second))


def keep_body(lhs, gain, gate, up, first, second):
    products(False, lhs, gain, gate, up, (first, second))


def send_partial(where, residual, far, attn_gain, gain, sums, gate, up):
    return call(
        send_body,
        (shaped((32, WIDTH), F32), shaped((2, 256, WIDTH), BF16))
        + tuple(shaped((128, width), BF16) for width in WIDTHS),
        [SM] + [VM] * 8,
        [pltpu.VMEM((2, 128, WIDTH), F32), pltpu.VMEM((4, 256, HD), F32)],
    )(where, residual, far, attn_gain, gain, *sums, gate, up)


def halve_body(send, *refs):
    ins, outs = refs[:4], refs[4:]
    rows = slice(64, 128) if send else slice(0, 64)
    for f in range(2):
        keep, other = ins[2 * f], ins[2 * f + 1]
        whole = keep[rows, : 2 * HALF] + other[rows, : 2 * HALF].astype(F32)
        outs[f][:, : 2 * HALF] = whole.astype(outs[f].dtype)
        if f == 0:
            squares = keep[rows, 2 * HALF :] + one_part(other[rows, 2 * HALF :])
            outs[0][:, 2 * HALF :] = two_parts(squares) if send else squares


def quarter_body(places, *refs):
    ins, outs = refs[:4], refs[4:]
    for k, out in zip(places, outs):
        rows = slice(gray(k) * 16, gray(k) * 16 + 16)
        for f in range(2):
            keep, other = ins[2 * f], ins[2 * f + 1]
            start = f * 2 * HALF
            whole = keep[rows, : 2 * HALF] + other[rows, : 2 * HALF].astype(F32)
            out[:, start : start + 2 * HALF] = whole.astype(out.dtype)
        squares = ins[0][rows, 2 * HALF :] + one_part(ins[1][rows, 2 * HALF :])
        out[:, 4 * HALF :] = squares if k == 0 else two_parts(squares)


def hidden_body(own, one, three, two, out):
    others = (one, two, three)
    squares = own[:, 4 * HALF :] + sum(one_part(other[:, 4 * HALF :]) for other in others)
    scale = lax.rsqrt(squares / D + EPSILON)[:, :1]
    for f in range(2):
        gate, up = (
            (own[:, columns] + sum(other[:, columns].astype(F32) for other in others)) * scale
            for columns in (slice(i * HALF, i * HALF + HALF) for i in (2 * f, 2 * f + 1))
        )
        out[:, f * HALF : f * HALF + HALF] = (gate / (1.0 + jnp.exp(-gate)) * up).astype(BF16)


def hidden_units(lhs, gain, gate, up, sends):
    moved = [swap_by_core(sends[0], 4, 1), swap_by_core(sends[1], 12, 3)]
    keeps = call(keep_body, tuple(shaped((128, width), F32) for width in WIDTHS), [VM] * 4)(lhs, gain, gate, up)
    parts = [keeps[0], moved[0], keeps[1], moved[1]]
    sends = call(
        functools.partial(halve_body, True), tuple(shaped((64, width), BF16) for width in WIDTHS), [VM] * 4
    )(*parts)
    moved = [swap_by_core(sends[0], 12, 3), swap_by_core(sends[1], 4, 1)]
    keeps = call(
        functools.partial(halve_body, False), tuple(shaped((64, width), F32) for width in WIDTHS), [VM] * 4
    )(*parts)
    parts = [keeps[0], moved[0], keeps[1], moved[1]]
    wide = 4 * HALF + HD
    sends = call(functools.partial(quarter_body, (1, 2, 3)), (shaped((16, wide), BF16),) * 3, [VM] * 4)(*parts)
    own = call(functools.partial(quarter_body, (0,)), shaped((16, wide), F32), [VM] * 4)(*parts)
    moved = [swap_by_core(sends[k - 1], k, 4 * k) for k in (1, 3, 2)]
    return call(hidden_body, shaped((16, UNITS), BF16), [VM] * 4)(own, *moved)


def stack_body(*refs):
    *pieces, out = refs
    rows = pieces[0].shape[0]
    for k, piece in enumerate(pieces):
        out[k * rows : k * rows + rows, :] = piece[...]


def down_body(where, *refs):
    pieces, (weight, send, lhs) = refs[:4], refs[4:]
    core = where[1] & 1
    for m in range(4):
        for k in range(4):
            step = jnp.where(core == 0, gray(m) * 4 + gray(k), gray(k) * 4 + gray(m))
            place = where[0] ^ step
            block = (place >> 1) ^ where[1]
            start = (block & 1) * 128 + (block >> 1) * 32 + (place & 1) * 16
            lhs[pl.ds(pl.multiple_of(start, 16), 16), :] = pieces[m][k * 16 : k * 16 + 16, :]
    send[...] = jnp.dot(lhs[128:, :], weight[...], preferred_element_type=F32).astype(BF16)


def own_body(lhs, weight, keep):
    keep[...] = jnp.dot(lhs[:128, :], weight[...], preferred_element_type=F32)


def down_partial(where, units, weight):
    pieces = [units] + [swap_by_core(units, k, 4 * k) for k in (1, 2, 3)]
    near = call(stack_body, shaped((64, UNITS), BF16), [VM] * 4)(*pieces)
    pieces = [near] + [swap_by_core(near, 4 * k, k) for k in (1, 2, 3)]
    send, lhs = call(
        down_body, (shaped((128, WIDTH), BF16), shaped((256, UNITS), BF16)), [SM] + [VM] * 5
    )(where, *pieces, weight)
    other = swap_gy(send, 1)
    return call(own_body, shaped((128, WIDTH), F32), [VM] * 2)(lhs, weight), other


def rotations(positions):
    frequency = jnp.exp(jnp.arange(HD // 2, dtype=F32) * (-2.0 / HD) * jnp.log(THETA))
    rows = []
    for t in range(2):
        angles = (positions + t).astype(F32) * frequency
        cosine, sine = jnp.cos(angles), jnp.sin(angles)
        rows += [jnp.concatenate([cosine, cosine]), jnp.concatenate([-sine, sine])]
    return jnp.stack(rows)


def per_device(
    inputs,
    positions,
    attn_gain,
    ffn_gain,
    qkv_weight,
    out_weight,
    gate_weight,
    up_weight,
    down_weight,
    k_cache,
    v_cache,
):
    gx, gy = lax.axis_index("gx"), lax.axis_index("gy")
    where = jnp.stack([gray(gx >> 2) * 4 + gray(gx & 3), gy]).astype(jnp.int32)
    angles = rotations(positions)
    attn_gain, ffn_gain = attn_gain.reshape(1, WIDTH), ffn_gain.reshape(1, WIDTH)

    twin = swap_gy(out_weight, 1)
    residual, near, far, attn_gain, qkv_weight, out_weight = gather_rows(
        inputs.reshape(32, WIDTH), attn_gain, qkv_weight, out_weight
    )
    partial = qkv_partial(where, near, far, attn_gain, qkv_weight, angles, twin)
    partial = partial.reshape(128, 24, HD)
    received = lax.all_to_all(partial, ("gx", "gy"), 0, 0, tiled=True).reshape(NX, NY, 24, HD)
    attended, new_kv = attend(angles, received, k_cache, v_cache)
    heads = lax.all_to_all(
        attended.reshape(64, 32, HD),
        ("gx", "gy"),
        0,
        0,
        axis_index_groups=[[i * NY + 2 * j + core for i in range(NX) for j in range(NY // 2)] for core in range(2)],
        tiled=True,
    )
    even_odd = sum_over_x(*out_partial(where, heads.reshape(64 * 32, HD), out_weight, twin))
    after_attn, lhs, *sends = send_partial(
        where, residual, far, attn_gain, ffn_gain, even_odd, gate_weight, up_weight
    )
    units = hidden_units(lhs, ffn_gain, gate_weight, up_weight, sends)
    outputs = add_ffn(after_attn, *down_partial(where, units, down_weight))
    return outputs.reshape(2, 16, WIDTH), new_kv


def solution(mesh):
    placed = (
        P(None, "gy", "gx"),
        P(("gx", "gy")),
        P("gx"),
        P("gx"),
        P("gx", "gy"),
        P("gy", "gx"),
        P("gx", "gy"),
        P("gx", "gy"),
        P("gy", "gx"),
        P(("gx", "gy"), None, None, None),
        P(("gx", "gy"), None, None, None),
    )
    return jax.shard_map(
        per_device,
        mesh=mesh,
        in_specs=placed,
        out_specs=(P(None, "gy", "gx"), P(("gx", "gy"), None, None, None)),
        check_vma=False,
    )
```

```python
import functools

import jax
import jax.numpy as jnp
from jax import lax
from jax.experimental import pallas as pl
from jax.experimental.pallas import tpu as pltpu
from jax.sharding import PartitionSpec as P

D = 8192
KVH = 8
HD = 128
CACHE = 1024
GQ = 8
EPSILON = 1e-05
THETA = 500000.0
NX = 16
NY = 8
WIDTH = 512
UNITS = 3584
HALF = UNITS // 2
WIDTHS = (2 * HALF + HD, 2 * HALF)
F32 = jnp.float32
BF16 = jnp.bfloat16
MIB = 1 << 20

VM = pl.BlockSpec(memory_space=pltpu.VMEM)
SM = pl.BlockSpec(memory_space=pltpu.SMEM)
HBM = pl.BlockSpec(memory_space=pltpu.HBM)
ANY = pl.BlockSpec(memory_space=pl.ANY)


def swap_gx(array, bits):
    return lax.ppermute(array, "gx", [(i, i ^ bits) for i in range(NX)])


def swap_gy(array, bits):
    return lax.ppermute(array, "gy", [(i, i ^ bits) for i in range(NY)])


def swap_by_core(array, first, second, axis="gx"):
    pairs = []
    for i in range(NX):
        for j in range(NY):
            bits = second if j & 1 else first
            pairs.append((i * NY + j, (i ^ bits) * NY + j if axis == "gx" else i * NY + (j ^ bits)))
    return lax.ppermute(array, ("gx", "gy"), pairs)


def gray(place):
    return ((place & 1) ^ (place >> 1)) * 2 + (place >> 1)


def call(body, outs, ins, scratch=(), limit=14, cost=0):
    cost = pl.CostEstimate(flops=0, bytes_accessed=cost, transcendentals=0) if cost else None
    return pl.pallas_call(
        body,
        out_shape=outs,
        in_specs=ins,
        out_specs=jax.tree.map(lambda _: VM, outs),
        scratch_shapes=list(scratch),
        compiler_params=pltpu.CompilerParams(vmem_limit_bytes=limit * MIB),
        cost_estimate=cost,
    )


def hbm(array):
    return pltpu.with_memory_space_constraint(array, pltpu.HBM)


def shaped(shape, dtype):
    return jax.ShapeDtypeStruct(shape, dtype)


def bring_body(count, *refs):
    ins, outs, sems = refs[:count], refs[count:-1], refs[-1]
    fetches = [pltpu.make_async_copy(a, b, sems.at[i]) for i, (a, b) in enumerate(zip(ins, outs))]
    for fetch in fetches:
        fetch.start()
    for fetch in fetches:
        fetch.wait()


def bring(arrays):
    size = sum(a.size * a.dtype.itemsize for a in arrays)
    outs = pl.pallas_call(
        functools.partial(bring_body, len(arrays)),
        out_shape=tuple(pltpu.VMEM(a.shape, a.dtype) for a in arrays),
        in_specs=[HBM] * len(arrays),
        out_specs=(VM,) * len(arrays),
        scratch_shapes=[pltpu.SemaphoreType.DMA((len(arrays),))],
        compiler_params=pltpu.CompilerParams(vmem_limit_bytes=14 * MIB),
        cost_estimate=pl.CostEstimate(flops=0, bytes_accessed=2 * size, transcendentals=0),
    )(*(hbm(a) for a in arrays))
    return [pltpu.with_memory_space_constraint(a, pltpu.VMEM) for a in outs]


def qkv_rows(source, gain, weight, rows):
    plain = source[...].astype(F32) / gain[...]
    squares = jnp.broadcast_to(jnp.sum(plain * plain, axis=1, keepdims=True), (128, HD))
    high = squares.astype(BF16).astype(F32)
    places = [(k, t, k * 32 + t * 16) for k in range(4) for t in range(2)]
    for k, t, start in places:
        rows[pl.ds(k * 384 + 20 + 2 * t, 16, stride=24), :] = high[start : start + 16]
        rows[pl.ds(k * 384 + 21 + 2 * t, 16, stride=24), :] = squares[start : start + 16] - high[start : start + 16]
    for pair in range(5):
        part = jnp.dot(source[...], weight[:, pair * 256 : pair * 256 + 256], preferred_element_type=F32)
        for j in (2 * pair, 2 * pair + 1):
            column = (j - 2 * pair) * HD
            for k, t, start in places:
                place = t * 8 + j if j < GQ else 16 + (j - GQ) * 2 + t
                rows[pl.ds(k * 384 + place, 16, stride=24), :] = part[start : start + 16, column : column + HD]


def near_body(near, gain, weight, out, rows):
    qkv_rows(near, gain, weight, rows)
    out[...] = rows[...].astype(BF16)


def qkv_body(where, earlier, far, gain, weight, angles, twin, out, rows):
    qkv_rows(far, gain, weight, rows)
    for k in range(4):
        part = slice(k * 384, k * 384 + 384)
        start = pl.multiple_of((where[1] ^ (2 * k)) * 384, 16)
        out[pl.ds(start, 384), :] = earlier[part, :]
        start = pl.multiple_of((where[1] ^ (2 * k + 1)) * 384, 16)
        out[pl.ds(start, 384), :] = rows[part, :].astype(BF16)


def qkv_partial(where, near, far, gain, weight, *order):
    scratch = [pltpu.VMEM((64 * 24, HD), F32)]
    earlier = call(near_body, shaped((64 * 24, HD), BF16), [VM] * 3, scratch)(near, gain, weight)
    return call(
        qkv_body, shaped((128 * 24, HD), BF16), [SM] + [VM] * 4 + [ANY] * 2, scratch
    )(where, earlier, far, gain, weight, *order)


def turn(vectors, cosine, sine):
    return vectors * cosine + pltpu.roll(vectors, HD // 2, vectors.ndim - 1) * sine


def attend_body(angles, received, keys, values, out, fresh, scores):
    total = received[0].astype(F32)
    for i in range(1, NX):
        total = total + received[i].astype(F32)
    squares = total[:, 20:24, :]
    scales = []
    for t in range(2):
        square = squares[:, 2 * t : 2 * t + 1, :] + squares[:, 2 * t + 1 : 2 * t + 2, :]
        scales.append(lax.rsqrt(square / D + EPSILON))
    cosines = [angles[2 * t : 2 * t + 1, :] for t in range(2)]
    sines = [angles[2 * t + 1 : 2 * t + 2, :] for t in range(2)]
    queries, new_keys, new_values = [], [], []
    for t in range(2):
        head = (total[:, 8 * t : 8 * t + 8, :] * scales[t]).astype(BF16).astype(F32)
        flat = turn(head.reshape(64, HD), cosines[t], sines[t])
        queries.append((flat * HD**-0.5).astype(BF16).astype(F32).reshape(8, 8, HD))
        key = (total[:, 16 + t : 17 + t, :] * scales[t]).astype(BF16).astype(F32).reshape(8, HD)
        new_keys.append(turn(key, cosines[t], sines[t]).astype(BF16))
        value = (total[:, 18 + t : 19 + t, :] * scales[t]).astype(BF16).reshape(8, HD)
        new_values.append(value)
        fresh[0, t, :, :HD] = new_keys[t]
        fresh[0, t, :, HD:] = value
    both = jnp.concatenate(queries, axis=1)
    both16 = both.astype(BF16)
    for g in range(KVH):
        scores[g * 16 : g * 16 + 16, :] = lax.dot_general(
            both16[g], keys[0, g], (((1,), (1,)), ((), ())), preferred_element_type=F32
        )
    extra = []
    step = lax.broadcasted_iota(jnp.int32, (KVH, 16, 1), 1) // GQ
    for t in range(2):
        dots = jnp.sum(both * new_keys[t].astype(F32).reshape(KVH, 1, HD), axis=2, keepdims=True)
        if t == 1:
            dots = jnp.where(step >= 1, dots, -3.0e38)
        extra.append(dots.reshape(128, 1))
    cached = scores[...]
    top = jnp.maximum(jnp.max(cached, axis=1, keepdims=True), jnp.maximum(extra[0], extra[1]))
    cached = jnp.exp(cached - top)
    extra = [jnp.exp(value - top) for value in extra]
    share = 1.0 / (jnp.sum(cached, axis=1, keepdims=True) + extra[0] + extra[1])
    probs = (cached * share).astype(BF16)
    extra = [(value * share).astype(BF16).astype(F32).reshape(KVH, 16, 1) for value in extra]
    for g in range(KVH):
        mixed = jnp.dot(probs[g * 16 : g * 16 + 16, :], values[0, g], preferred_element_type=F32)
        for t in range(2):
            mixed = mixed + extra[t][g] * new_values[t][g : g + 1, :].astype(F32)
        mixed = mixed.astype(BF16)
        for i in range(NX):
            out[i, g] = mixed


def attend(angles, received, keys, values):
    return call(
        attend_body,
        (shaped((NX, KVH, 16, HD), BF16), shaped((1, 2, KVH, 2 * HD), BF16)),
        [VM, VM, VM, VM],
        [pltpu.VMEM((KVH * 16, CACHE), F32)],
    )(angles, received, keys, values)


def out_body(where, received, weight, twin, total, send, wide, lhs):
    wide[...] = received[...].astype(F32)
    for other in range(2):
        core = (where[1] & 1) ^ other
        for t in range(2):
            for h in range(GQ):
                column = (other * GQ + h) * HD
                lhs[t * 64 : t * 64 + 64, column : column + HD] = wide[
                    pl.ds(core * 16 + t * 8 + h, 64, stride=32), :
                ].astype(BF16)
    half = GQ * HD
    part = jnp.dot(lhs[:, :half], weight[...], preferred_element_type=F32)
    part = part + jnp.dot(lhs[:, half:], twin[...], preferred_element_type=F32)
    total[...] = part
    send[...] = part.astype(BF16)


def out_partial(where, received, mine, twin):
    return call(
        out_body,
        (shaped((128, WIDTH), F32), shaped((128, WIDTH), BF16)),
        [SM, VM, VM, VM],
        [pltpu.VMEM((64 * 32, HD), F32), pltpu.VMEM((128, 2 * GQ * HD), BF16)],
    )(where, received, mine, twin)


def add_body(whole, three, one, two, mine):
    total = whole[...] + (one[...].astype(F32) + two[...].astype(F32) + three[...].astype(F32))
    mine[...] = total.astype(BF16)


def sum_over_x(whole, sent):
    others = [swap_gy(sent, 2 * k) for k in (3, 1, 2)]
    mine = call(add_body, shaped((128, WIDTH), BF16), [VM] * 4)(whole, *others)
    return mine, swap_gy(mine, 1)


def split_body(keep, other, own, *sends):
    whole = keep[...] + other[...].astype(F32)
    own[...] = whole[:32]
    for k, send in enumerate(sends):
        send[...] = whole[32 * k + 32 : 32 * k + 64].astype(BF16)


def final_body(residual, own, two, one, three, out):
    out[...] = residual[...] + (own[...] + one[...].astype(F32) + two[...].astype(F32) + three[...].astype(F32))


def add_ffn(after, keep, other):
    own, *sends = call(
        split_body,
        (shaped((32, WIDTH), F32),) + (shaped((32, WIDTH), BF16),) * 3,
        [VM, VM],
    )(keep, other)
    pieces = [swap_gy(sends[k - 1], 2 * k) for k in (2, 1, 3)]
    return call(final_body, shaped((32, WIDTH), F32), [VM] * 5)(after, own, *pieces)


def rows_body(own, one, two, three, gain, residual, scaled):
    for k, piece in enumerate((own, one, two, three)):
        rows = slice(k * 32, k * 32 + 32)
        residual[rows, :] = piece[...]
        scaled[rows, :] = (piece[...] * gain[...]).astype(BF16)


def gather_rows(own, gain, *weights):
    pieces = [swap_gy(own, 2 * k) for k in (1, 2, 3)]
    own, gain, *weights = bring((own, gain, *weights))
    residual, near = call(
        rows_body, (shaped((128, WIDTH), F32), shaped((128, WIDTH), BF16)), [VM] * 5
    )(own, *pieces, gain)
    return residual, near, swap_gy(near, 1), gain, *weights


def two_parts(squares):
    high = squares.astype(BF16).astype(F32)
    first = lax.broadcasted_iota(jnp.int32, squares.shape, 1) < HD // 2
    return jnp.where(first, high, squares - high).astype(BF16)


def one_part(parts):
    wide = parts.astype(F32)
    return wide + pltpu.roll(wide, HD // 2, 1)


def place_of(flow, core, chunk):
    turned = jnp.where(core == 0, chunk, ((chunk << 2) | (chunk >> 2)) & 15)
    if flow == 1:
        turned = (turned & 3) | ((turned & 4) << 1) | ((turned & 8) >> 1)
    return turned


def products(send, lhs, gain, gate, up, outs):
    rows = slice(128, 256) if send else slice(0, 128)
    plain = lhs[0, rows, :].astype(F32) / gain[...]
    squares = jnp.broadcast_to(jnp.sum(plain * plain, axis=1, keepdims=True), (128, HD))
    outs[0][:, 2 * HALF :] = two_parts(squares) if send else squares
    for f in range(2):
        for i, weight in enumerate((gate, up)):
            part = jnp.dot(lhs[f, rows, :], weight[:, f * HALF : f * HALF + HALF], preferred_element_type=F32)
            outs[f][:, i * HALF : i * HALF + HALF] = part.astype(outs[f].dtype)


def send_body(where, residual, far, attn_gain, gain, mine, twin, gate, up, after, lhs, first, second, sums, attention):
    core = where[1] & 1
    sums[0] = jnp.where(core == 0, mine[...].astype(F32), twin[...].astype(F32))
    sums[1] = jnp.where(core == 0, twin[...].astype(F32), mine[...].astype(F32))
    for chunk in range(16):
        block = where[1] ^ (2 * ((chunk >> 1) & 3) + (chunk >> 3))
        start = pl.multiple_of((chunk & 1) * 64 + block * 8, 8)
        for odd in range(2):
            for q in range(4):
                attention[q, pl.ds(chunk * 16 + odd, 8, stride=2), :] = sums[
                    odd, pl.ds(start, 8), q * 128 : q * 128 + 128
                ]
    for chunk in range(16):
        rows = slice(chunk * 16, chunk * 16 + 16)
        if chunk < 8:
            whole = residual[rows, :]
        else:
            whole = far[chunk * 16 - 128 : chunk * 16 - 112, :].astype(F32) / attn_gain[...]
        whole = whole + jnp.concatenate([attention[q, rows, :] for q in range(4)], axis=1)
        if chunk < 2:
            after[rows, :] = whole
        normed = (whole * gain[...]).astype(BF16)
        block = where[1] ^ (2 * ((chunk >> 1) & 3) + (chunk >> 3))
        for f in range(2):
            place = place_of(f, core, (2 * block + (chunk & 1)) ^ where[0])
            lhs[f, pl.ds(pl.multiple_of(place * 16, 16), 16), :] = normed
    products(True, lhs, gain, gate, up, (first, second))


def keep_body(lhs, gain, gate, up, first, second):
    products(False, lhs, gain, gate, up, (first, second))


def send_partial(where, residual, far, attn_gain, gain, sums, gate, up):
    return call(
        send_body,
        (shaped((32, WIDTH), F32), shaped((2, 256, WIDTH), BF16))
        + tuple(shaped((128, width), BF16) for width in WIDTHS),
        [SM] + [VM] * 8,
        [pltpu.VMEM((2, 128, WIDTH), F32), pltpu.VMEM((4, 256, HD), F32)],
    )(where, residual, far, attn_gain, gain, *sums, gate, up)


def halve_body(send, *refs):
    ins, outs = refs[:4], refs[4:]
    rows = slice(64, 128) if send else slice(0, 64)
    for f in range(2):
        keep, other = ins[2 * f], ins[2 * f + 1]
        whole = keep[rows, : 2 * HALF] + other[rows, : 2 * HALF].astype(F32)
        outs[f][:, : 2 * HALF] = whole.astype(outs[f].dtype)
        if f == 0:
            squares = keep[rows, 2 * HALF :] + one_part(other[rows, 2 * HALF :])
            outs[0][:, 2 * HALF :] = two_parts(squares) if send else squares


def quarter_body(places, *refs):
    ins, outs = refs[:4], refs[4:]
    for k, out in zip(places, outs):
        rows = slice(gray(k) * 16, gray(k) * 16 + 16)
        for f in range(2):
            keep, other = ins[2 * f], ins[2 * f + 1]
            start = f * 2 * HALF
            whole = keep[rows, : 2 * HALF] + other[rows, : 2 * HALF].astype(F32)
            out[:, start : start + 2 * HALF] = whole.astype(out.dtype)
        squares = ins[0][rows, 2 * HALF :] + one_part(ins[1][rows, 2 * HALF :])
        out[:, 4 * HALF :] = squares if k == 0 else two_parts(squares)


def hidden_body(own, two, one, three, out):
    others = (one, two, three)
    squares = own[:, 4 * HALF :] + sum(one_part(other[:, 4 * HALF :]) for other in others)
    scale = lax.rsqrt(squares / D + EPSILON)[:, :1]
    for f in range(2):
        gate, up = (
            (own[:, columns] + sum(other[:, columns].astype(F32) for other in others)) * scale
            for columns in (slice(i * HALF, i * HALF + HALF) for i in (2 * f, 2 * f + 1))
        )
        out[:, f * HALF : f * HALF + HALF] = (gate / (1.0 + jnp.exp(-gate)) * up).astype(BF16)


def hidden_units(lhs, gain, gate, up, sends):
    moved = [swap_by_core(sends[0], 4, 1), swap_by_core(sends[1], 12, 3)]
    keeps = call(keep_body, tuple(shaped((128, width), F32) for width in WIDTHS), [VM] * 4)(lhs, gain, gate, up)
    parts = [keeps[0], moved[0], keeps[1], moved[1]]
    sends = call(
        functools.partial(halve_body, True), tuple(shaped((64, width), BF16) for width in WIDTHS), [VM] * 4
    )(*parts)
    moved = [swap_by_core(sends[0], 12, 3), swap_by_core(sends[1], 4, 1)]
    keeps = call(
        functools.partial(halve_body, False), tuple(shaped((64, width), F32) for width in WIDTHS), [VM] * 4
    )(*parts)
    parts = [keeps[0], moved[0], keeps[1], moved[1]]
    wide = 4 * HALF + HD
    sends = call(functools.partial(quarter_body, (1, 2, 3)), (shaped((16, wide), BF16),) * 3, [VM] * 4)(*parts)
    own = call(functools.partial(quarter_body, (0,)), shaped((16, wide), F32), [VM] * 4)(*parts)
    moved = [swap_by_core(sends[k - 1], k, 4 * k) for k in (2, 1, 3)]
    return call(hidden_body, shaped((16, UNITS), BF16), [VM] * 4)(own, *moved)


def stack_body(*refs):
    *pieces, out = refs
    rows = pieces[0].shape[0]
    for k, piece in enumerate(pieces):
        out[k * rows : k * rows + rows, :] = piece[...]


def down_body(where, own, three, one, two, weight, send, lhs):
    pieces = (own, one, two, three)
    core = where[1] & 1
    for m in range(4):
        for k in range(4):
            step = jnp.where(core == 0, gray(m) * 4 + gray(k), gray(k) * 4 + gray(m))
            place = where[0] ^ step
            block = (place >> 1) ^ where[1]
            start = (block & 1) * 128 + (block >> 1) * 32 + (place & 1) * 16
            lhs[pl.ds(pl.multiple_of(start, 16), 16), :] = pieces[m][k * 16 : k * 16 + 16, :]
    send[...] = jnp.dot(lhs[128:, :], weight[...], preferred_element_type=F32).astype(BF16)


def own_body(lhs, weight, keep):
    keep[...] = jnp.dot(lhs[:128, :], weight[...], preferred_element_type=F32)


def down_partial(where, units, weight):
    pieces = [units] + [swap_by_core(units, k, 4 * k) for k in (1, 2, 3)]
    near = call(stack_body, shaped((64, UNITS), BF16), [VM] * 4)(*pieces)
    pieces = [near] + [swap_by_core(near, 4 * k, k) for k in (3, 1, 2)]
    send, lhs = call(
        down_body, (shaped((128, WIDTH), BF16), shaped((256, UNITS), BF16)), [SM] + [VM] * 5
    )(where, *pieces, weight)
    other = swap_gy(send, 1)
    return call(own_body, shaped((128, WIDTH), F32), [VM] * 2)(lhs, weight), other


def rotations(positions):
    frequency = jnp.exp(jnp.arange(HD // 2, dtype=F32) * (-2.0 / HD) * jnp.log(THETA))
    rows = []
    for t in range(2):
        angles = (positions + t).astype(F32) * frequency
        cosine, sine = jnp.cos(angles), jnp.sin(angles)
        rows += [jnp.concatenate([cosine, cosine]), jnp.concatenate([-sine, sine])]
    return jnp.stack(rows)


def per_device(
    inputs,
    positions,
    attn_gain,
    ffn_gain,
    qkv_weight,
    out_weight,
    gate_weight,
    up_weight,
    down_weight,
    k_cache,
    v_cache,
):
    gx, gy = lax.axis_index("gx"), lax.axis_index("gy")
    where = jnp.stack([gray(gx >> 2) * 4 + gray(gx & 3), gy]).astype(jnp.int32)
    angles = rotations(positions)
    attn_gain, ffn_gain = attn_gain.reshape(1, WIDTH), ffn_gain.reshape(1, WIDTH)

    twin = swap_gy(out_weight, 1)
    residual, near, far, attn_gain, qkv_weight, out_weight = gather_rows(
        inputs.reshape(32, WIDTH), attn_gain, qkv_weight, out_weight
    )
    partial = qkv_partial(where, near, far, attn_gain, qkv_weight, angles, twin)
    partial = partial.reshape(128, 24, HD)
    received = lax.all_to_all(partial, ("gx", "gy"), 0, 0, tiled=True).reshape(NX, NY, 24, HD)
    attended, new_kv = attend(angles, received, k_cache, v_cache)
    heads = lax.all_to_all(
        attended.reshape(64, 32, HD),
        ("gx", "gy"),
        0,
        0,
        axis_index_groups=[[i * NY + 2 * j + core for i in range(NX) for j in range(NY // 2)] for core in range(2)],
        tiled=True,
    )
    even_odd = sum_over_x(*out_partial(where, heads.reshape(64 * 32, HD), out_weight, twin))
    after_attn, lhs, *sends = send_partial(
        where, residual, far, attn_gain, ffn_gain, even_odd, gate_weight, up_weight
    )
    units = hidden_units(lhs, ffn_gain, gate_weight, up_weight, sends)
    outputs = add_ffn(after_attn, *down_partial(where, units, down_weight))
    return outputs.reshape(2, 16, WIDTH), new_kv


def solution(mesh):
    placed = (
        P(None, "gy", "gx"),
        P(("gx", "gy")),
        P("gx"),
        P("gx"),
        P("gx", "gy"),
        P("gy", "gx"),
        P("gx", "gy"),
        P("gx", "gy"),
        P("gy", "gx"),
        P(("gx", "gy"), None, None, None),
        P(("gx", "gy"), None, None, None),
    )
    return jax.shard_map(
        per_device,
        mesh=mesh,
        in_specs=placed,
        out_specs=(P(None, "gy", "gx"), P(("gx", "gy"), None, None, None)),
        check_vma=False,
    )
```

```python
import functools

import jax
import jax.numpy as jnp
from jax import lax
from jax.experimental import pallas as pl
from jax.experimental.pallas import tpu as pltpu
from jax.sharding import PartitionSpec as P

D = 8192
KVH = 8
HD = 128
CACHE = 1024
GQ = 8
EPSILON = 1e-05
THETA = 500000.0
NX = 16
NY = 8
WIDTH = 512
UNITS = 3584
HALF = UNITS // 2
WIDTHS = (2 * HALF + HD, 2 * HALF)
F32 = jnp.float32
BF16 = jnp.bfloat16
MIB = 1 << 20

VM = pl.BlockSpec(memory_space=pltpu.VMEM)
SM = pl.BlockSpec(memory_space=pltpu.SMEM)
HBM = pl.BlockSpec(memory_space=pltpu.HBM)
ANY = pl.BlockSpec(memory_space=pl.ANY)


def swap_gx(array, bits):
    return lax.ppermute(array, "gx", [(i, i ^ bits) for i in range(NX)])


def swap_gy(array, bits):
    return lax.ppermute(array, "gy", [(i, i ^ bits) for i in range(NY)])


def swap_by_core(array, first, second, axis="gx"):
    pairs = []
    for i in range(NX):
        for j in range(NY):
            bits = second if j & 1 else first
            pairs.append((i * NY + j, (i ^ bits) * NY + j if axis == "gx" else i * NY + (j ^ bits)))
    return lax.ppermute(array, ("gx", "gy"), pairs)


def gray(place):
    return ((place & 1) ^ (place >> 1)) * 2 + (place >> 1)


def call(body, outs, ins, scratch=(), limit=14, cost=0):
    cost = pl.CostEstimate(flops=0, bytes_accessed=cost, transcendentals=0) if cost else None
    return pl.pallas_call(
        body,
        out_shape=outs,
        in_specs=ins,
        out_specs=jax.tree.map(lambda _: VM, outs),
        scratch_shapes=list(scratch),
        compiler_params=pltpu.CompilerParams(vmem_limit_bytes=limit * MIB),
        cost_estimate=cost,
    )


def hbm(array):
    return pltpu.with_memory_space_constraint(array, pltpu.HBM)


def shaped(shape, dtype):
    return jax.ShapeDtypeStruct(shape, dtype)


def bring_body(count, *refs):
    ins, outs, sems = refs[:count], refs[count:-1], refs[-1]
    fetches = [pltpu.make_async_copy(a, b, sems.at[i]) for i, (a, b) in enumerate(zip(ins, outs))]
    for fetch in fetches:
        fetch.start()
    for fetch in fetches:
        fetch.wait()


def bring(arrays):
    size = sum(a.size * a.dtype.itemsize for a in arrays)
    outs = pl.pallas_call(
        functools.partial(bring_body, len(arrays)),
        out_shape=tuple(pltpu.VMEM(a.shape, a.dtype) for a in arrays),
        in_specs=[HBM] * len(arrays),
        out_specs=(VM,) * len(arrays),
        scratch_shapes=[pltpu.SemaphoreType.DMA((len(arrays),))],
        compiler_params=pltpu.CompilerParams(vmem_limit_bytes=14 * MIB),
        cost_estimate=pl.CostEstimate(flops=0, bytes_accessed=2 * size, transcendentals=0),
    )(*(hbm(a) for a in arrays))
    return [pltpu.with_memory_space_constraint(a, pltpu.VMEM) for a in outs]


def qkv_rows(source, gain, weight, rows):
    plain = source[...].astype(F32) / gain[...]
    squares = jnp.broadcast_to(jnp.sum(plain * plain, axis=1, keepdims=True), (128, HD))
    high = squares.astype(BF16).astype(F32)
    places = [(k, t, k * 32 + t * 16) for k in range(4) for t in range(2)]
    for k, t, start in places:
        rows[pl.ds(k * 384 + 20 + 2 * t, 16, stride=24), :] = high[start : start + 16]
        rows[pl.ds(k * 384 + 21 + 2 * t, 16, stride=24), :] = squares[start : start + 16] - high[start : start + 16]
    for pair in range(5):
        part = jnp.dot(source[...], weight[:, pair * 256 : pair * 256 + 256], preferred_element_type=F32)
        for j in (2 * pair, 2 * pair + 1):
            column = (j - 2 * pair) * HD
            for k, t, start in places:
                place = t * 8 + j if j < GQ else 16 + (j - GQ) * 2 + t
                rows[pl.ds(k * 384 + place, 16, stride=24), :] = part[start : start + 16, column : column + HD]


def near_body(near, gain, weight, out, rows):
    qkv_rows(near, gain, weight, rows)
    out[...] = rows[...].astype(BF16)


def qkv_body(where, earlier, far, gain, weight, angles, twin, out, rows):
    qkv_rows(far, gain, weight, rows)
    for k in range(4):
        part = slice(k * 384, k * 384 + 384)
        start = pl.multiple_of((where[1] ^ (2 * k)) * 384, 16)
        out[pl.ds(start, 384), :] = earlier[part, :]
        start = pl.multiple_of((where[1] ^ (2 * k + 1)) * 384, 16)
        out[pl.ds(start, 384), :] = rows[part, :].astype(BF16)


def qkv_partial(where, near, far, gain, weight, *order):
    scratch = [pltpu.VMEM((64 * 24, HD), F32)]
    earlier = call(near_body, shaped((64 * 24, HD), BF16), [VM] * 3, scratch)(near, gain, weight)
    return call(
        qkv_body, shaped((128 * 24, HD), BF16), [SM] + [VM] * 4 + [ANY] * 2, scratch
    )(where, earlier, far, gain, weight, *order)


def turn(vectors, cosine, sine):
    return vectors * cosine + pltpu.roll(vectors, HD // 2, vectors.ndim - 1) * sine


def attend_body(angles, received, keys, values, out, fresh, scores):
    total = received[0].astype(F32)
    for i in range(1, NX):
        total = total + received[i].astype(F32)
    squares = total[:, 20:24, :]
    scales = []
    for t in range(2):
        square = squares[:, 2 * t : 2 * t + 1, :] + squares[:, 2 * t + 1 : 2 * t + 2, :]
        scales.append(lax.rsqrt(square / D + EPSILON))
    cosines = [angles[2 * t : 2 * t + 1, :] for t in range(2)]
    sines = [angles[2 * t + 1 : 2 * t + 2, :] for t in range(2)]
    queries, new_keys, new_values = [], [], []
    for t in range(2):
        head = (total[:, 8 * t : 8 * t + 8, :] * scales[t]).astype(BF16).astype(F32)
        flat = turn(head.reshape(64, HD), cosines[t], sines[t])
        queries.append((flat * HD**-0.5).astype(BF16).astype(F32).reshape(8, 8, HD))
        key = (total[:, 16 + t : 17 + t, :] * scales[t]).astype(BF16).astype(F32).reshape(8, HD)
        new_keys.append(turn(key, cosines[t], sines[t]).astype(BF16))
        value = (total[:, 18 + t : 19 + t, :] * scales[t]).astype(BF16).reshape(8, HD)
        new_values.append(value)
        fresh[0, t, :, :HD] = new_keys[t]
        fresh[0, t, :, HD:] = value
    both = jnp.concatenate(queries, axis=1)
    both16 = both.astype(BF16)
    for g in range(KVH):
        scores[g * 16 : g * 16 + 16, :] = lax.dot_general(
            both16[g], keys[0, g], (((1,), (1,)), ((), ())), preferred_element_type=F32
        )
    extra = []
    step = lax.broadcasted_iota(jnp.int32, (KVH, 16, 1), 1) // GQ
    for t in range(2):
        dots = jnp.sum(both * new_keys[t].astype(F32).reshape(KVH, 1, HD), axis=2, keepdims=True)
        if t == 1:
            dots = jnp.where(step >= 1, dots, -3.0e38)
        extra.append(dots.reshape(128, 1))
    cached = scores[...]
    top = jnp.maximum(jnp.max(cached, axis=1, keepdims=True), jnp.maximum(extra[0], extra[1]))
    cached = jnp.exp(cached - top)
    extra = [jnp.exp(value - top) for value in extra]
    share = 1.0 / (jnp.sum(cached, axis=1, keepdims=True) + extra[0] + extra[1])
    probs = (cached * share).astype(BF16)
    extra = [(value * share).astype(BF16).astype(F32).reshape(KVH, 16, 1) for value in extra]
    for g in range(KVH):
        mixed = jnp.dot(probs[g * 16 : g * 16 + 16, :], values[0, g], preferred_element_type=F32)
        for t in range(2):
            mixed = mixed + extra[t][g] * new_values[t][g : g + 1, :].astype(F32)
        mixed = mixed.astype(BF16)
        for i in range(NX):
            out[i, g] = mixed


def attend(angles, received, keys, values):
    return call(
        attend_body,
        (shaped((NX, KVH, 16, HD), BF16), shaped((1, 2, KVH, 2 * HD), BF16)),
        [VM, VM, VM, VM],
        [pltpu.VMEM((KVH * 16, CACHE), F32)],
    )(angles, received, keys, values)


def out_body(where, received, weight, twin, total, send, wide, lhs):
    wide[...] = received[...].astype(F32)
    for other in range(2):
        core = (where[1] & 1) ^ other
        for t in range(2):
            for h in range(GQ):
                column = (other * GQ + h) * HD
                lhs[t * 64 : t * 64 + 64, column : column + HD] = wide[
                    pl.ds(core * 16 + t * 8 + h, 64, stride=32), :
                ].astype(BF16)
    half = GQ * HD
    part = jnp.dot(lhs[:, :half], weight[...], preferred_element_type=F32)
    part = part + jnp.dot(lhs[:, half:], twin[...], preferred_element_type=F32)
    total[...] = part
    send[...] = part.astype(BF16)


def out_partial(where, received, mine, twin):
    return call(
        out_body,
        (shaped((128, WIDTH), F32), shaped((128, WIDTH), BF16)),
        [SM, VM, VM, VM],
        [pltpu.VMEM((64 * 32, HD), F32), pltpu.VMEM((128, 2 * GQ * HD), BF16)],
    )(where, received, mine, twin)


def add_body(whole, three, one, two, mine):
    total = whole[...] + (one[...].astype(F32) + two[...].astype(F32) + three[...].astype(F32))
    mine[...] = total.astype(BF16)


def sum_over_x(whole, sent):
    others = [swap_gy(sent, 2 * k) for k in (3, 1, 2)]
    mine = call(add_body, shaped((128, WIDTH), BF16), [VM] * 4)(whole, *others)
    return mine, swap_gy(mine, 1)


def split_body(keep, other, own, *sends):
    whole = keep[...] + other[...].astype(F32)
    own[...] = whole[:32]
    for k, send in enumerate(sends):
        send[...] = whole[32 * k + 32 : 32 * k + 64].astype(BF16)


def final_body(residual, own, two, one, three, out):
    out[...] = residual[...] + (own[...] + one[...].astype(F32) + two[...].astype(F32) + three[...].astype(F32))


def add_ffn(after, keep, other):
    own, *sends = call(
        split_body,
        (shaped((32, WIDTH), F32),) + (shaped((32, WIDTH), BF16),) * 3,
        [VM, VM],
    )(keep, other)
    pieces = [swap_gy(sends[k - 1], 2 * k) for k in (2, 1, 3)]
    return call(final_body, shaped((32, WIDTH), F32), [VM] * 5)(after, own, *pieces)


def rows_body(own, one, two, three, gain, scaled):
    for k, piece in enumerate((own, one, two, three)):
        rows = slice(k * 32, k * 32 + 32)
        scaled[rows, :] = (piece[...] * gain[...]).astype(BF16)


def gather_rows(own, gain, *weights):
    pieces = [swap_gy(own, 2 * k) for k in (1, 2, 3)]
    own, gain, *weights = bring((own, gain, *weights))
    near = call(rows_body, shaped((128, WIDTH), BF16), [VM] * 5)(own, *pieces, gain)
    return (own, *pieces), near, swap_gy(near, 1), gain, *weights


def two_parts(squares):
    high = squares.astype(BF16).astype(F32)
    first = lax.broadcasted_iota(jnp.int32, squares.shape, 1) < HD // 2
    return jnp.where(first, high, squares - high).astype(BF16)


def one_part(parts):
    wide = parts.astype(F32)
    return wide + pltpu.roll(wide, HD // 2, 1)


def place_of(flow, core, chunk):
    turned = jnp.where(core == 0, chunk, ((chunk << 2) | (chunk >> 2)) & 15)
    if flow == 1:
        turned = (turned & 3) | ((turned & 4) << 1) | ((turned & 8) >> 1)
    return turned


def products(send, lhs, gain, gate, up, outs):
    rows = slice(128, 256) if send else slice(0, 128)
    plain = lhs[0, rows, :].astype(F32) / gain[...]
    squares = jnp.broadcast_to(jnp.sum(plain * plain, axis=1, keepdims=True), (128, HD))
    outs[0][:, 2 * HALF :] = two_parts(squares) if send else squares
    for f in range(2):
        for i, weight in enumerate((gate, up)):
            part = jnp.dot(lhs[f, rows, :], weight[:, f * HALF : f * HALF + HALF], preferred_element_type=F32)
            outs[f][:, i * HALF : i * HALF + HALF] = part.astype(outs[f].dtype)


def send_body(where, *refs):
    residual, refs = refs[:4], refs[4:]
    far, attn_gain, gain, mine, twin, gate, up, after, lhs, first, second, sums, attention = refs
    core = where[1] & 1
    sums[0] = jnp.where(core == 0, mine[...].astype(F32), twin[...].astype(F32))
    sums[1] = jnp.where(core == 0, twin[...].astype(F32), mine[...].astype(F32))
    for chunk in range(16):
        block = where[1] ^ (2 * ((chunk >> 1) & 3) + (chunk >> 3))
        start = pl.multiple_of((chunk & 1) * 64 + block * 8, 8)
        for odd in range(2):
            for q in range(4):
                attention[q, pl.ds(chunk * 16 + odd, 8, stride=2), :] = sums[
                    odd, pl.ds(start, 8), q * 128 : q * 128 + 128
                ]
    for chunk in range(16):
        rows = slice(chunk * 16, chunk * 16 + 16)
        if chunk < 8:
            whole = residual[chunk // 2][chunk % 2 * 16 : chunk % 2 * 16 + 16, :]
        else:
            whole = far[chunk * 16 - 128 : chunk * 16 - 112, :].astype(F32) / attn_gain[...]
        whole = whole + jnp.concatenate([attention[q, rows, :] for q in range(4)], axis=1)
        if chunk < 2:
            after[rows, :] = whole
        normed = (whole * gain[...]).astype(BF16)
        block = where[1] ^ (2 * ((chunk >> 1) & 3) + (chunk >> 3))
        for f in range(2):
            place = place_of(f, core, (2 * block + (chunk & 1)) ^ where[0])
            lhs[f, pl.ds(pl.multiple_of(place * 16, 16), 16), :] = normed
    products(True, lhs, gain, gate, up, (first, second))


def keep_body(lhs, gain, gate, up, first, second):
    products(False, lhs, gain, gate, up, (first, second))


def send_partial(where, residual, far, attn_gain, gain, sums, gate, up):
    return call(
        send_body,
        (shaped((32, WIDTH), F32), shaped((2, 256, WIDTH), BF16))
        + tuple(shaped((128, width), BF16) for width in WIDTHS),
        [SM] + [VM] * 11,
        [pltpu.VMEM((2, 128, WIDTH), F32), pltpu.VMEM((4, 256, HD), F32)],
    )(where, *residual, far, attn_gain, gain, *sums, gate, up)


def halve_body(send, *refs):
    ins, outs = refs[:4], refs[4:]
    rows = slice(64, 128) if send else slice(0, 64)
    for f in range(2):
        keep, other = ins[2 * f], ins[2 * f + 1]
        whole = keep[rows, : 2 * HALF] + other[rows, : 2 * HALF].astype(F32)
        outs[f][:, : 2 * HALF] = whole.astype(outs[f].dtype)
        if f == 0:
            squares = keep[rows, 2 * HALF :] + one_part(other[rows, 2 * HALF :])
            outs[0][:, 2 * HALF :] = two_parts(squares) if send else squares


def quarter_body(places, *refs):
    ins, outs = refs[:4], refs[4:]
    for k, out in zip(places, outs):
        rows = slice(gray(k) * 16, gray(k) * 16 + 16)
        for f in range(2):
            keep, other = ins[2 * f], ins[2 * f + 1]
            start = f * 2 * HALF
            whole = keep[rows, : 2 * HALF] + other[rows, : 2 * HALF].astype(F32)
            out[:, start : start + 2 * HALF] = whole.astype(out.dtype)
        squares = ins[0][rows, 2 * HALF :] + one_part(ins[1][rows, 2 * HALF :])
        out[:, 4 * HALF :] = squares if k == 0 else two_parts(squares)


def hidden_body(own, two, one, three, out):
    others = (one, two, three)
    squares = own[:, 4 * HALF :] + sum(one_part(other[:, 4 * HALF :]) for other in others)
    scale = lax.rsqrt(squares / D + EPSILON)[:, :1]
    for f in range(2):
        gate, up = (
            (own[:, columns] + sum(other[:, columns].astype(F32) for other in others)) * scale
            for columns in (slice(i * HALF, i * HALF + HALF) for i in (2 * f, 2 * f + 1))
        )
        out[:, f * HALF : f * HALF + HALF] = (gate / (1.0 + jnp.exp(-gate)) * up).astype(BF16)


def hidden_units(lhs, gain, gate, up, sends):
    moved = [swap_by_core(sends[0], 4, 1), swap_by_core(sends[1], 12, 3)]
    keeps = call(keep_body, tuple(shaped((128, width), F32) for width in WIDTHS), [VM] * 4)(lhs, gain, gate, up)
    parts = [keeps[0], moved[0], keeps[1], moved[1]]
    sends = call(
        functools.partial(halve_body, True), tuple(shaped((64, width), BF16) for width in WIDTHS), [VM] * 4
    )(*parts)
    moved = [swap_by_core(sends[0], 12, 3), swap_by_core(sends[1], 4, 1)]
    keeps = call(
        functools.partial(halve_body, False), tuple(shaped((64, width), F32) for width in WIDTHS), [VM] * 4
    )(*parts)
    parts = [keeps[0], moved[0], keeps[1], moved[1]]
    wide = 4 * HALF + HD
    sends = call(functools.partial(quarter_body, (1, 2, 3)), (shaped((16, wide), BF16),) * 3, [VM] * 4)(*parts)
    own = call(functools.partial(quarter_body, (0,)), shaped((16, wide), F32), [VM] * 4)(*parts)
    moved = [swap_by_core(sends[k - 1], k, 4 * k) for k in (2, 1, 3)]
    return call(hidden_body, shaped((16, UNITS), BF16), [VM] * 4)(own, *moved)


def stack_body(*refs):
    *pieces, out = refs
    rows = pieces[0].shape[0]
    for k, piece in enumerate(pieces):
        out[k * rows : k * rows + rows, :] = piece[...]


def down_body(where, own, three, one, two, weight, send, lhs):
    pieces = (own, one, two, three)
    core = where[1] & 1
    for m in range(4):
        for k in range(4):
            step = jnp.where(core == 0, gray(m) * 4 + gray(k), gray(k) * 4 + gray(m))
            place = where[0] ^ step
            block = (place >> 1) ^ where[1]
            start = (block & 1) * 128 + (block >> 1) * 32 + (place & 1) * 16
            lhs[pl.ds(pl.multiple_of(start, 16), 16), :] = pieces[m][k * 16 : k * 16 + 16, :]
    send[...] = jnp.dot(lhs[128:, :], weight[...], preferred_element_type=F32).astype(BF16)


def own_body(lhs, weight, keep):
    keep[...] = jnp.dot(lhs[:128, :], weight[...], preferred_element_type=F32)


def down_partial(where, units, weight):
    pieces = [units] + [swap_by_core(units, k, 4 * k) for k in (1, 2, 3)]
    near = call(stack_body, shaped((64, UNITS), BF16), [VM] * 4)(*pieces)
    pieces = [near] + [swap_by_core(near, 4 * k, k) for k in (3, 1, 2)]
    send, lhs = call(
        down_body, (shaped((128, WIDTH), BF16), shaped((256, UNITS), BF16)), [SM] + [VM] * 5
    )(where, *pieces, weight)
    other = swap_gy(send, 1)
    return call(own_body, shaped((128, WIDTH), F32), [VM] * 2)(lhs, weight), other


def rotations(positions):
    frequency = jnp.exp(jnp.arange(HD // 2, dtype=F32) * (-2.0 / HD) * jnp.log(THETA))
    rows = []
    for t in range(2):
        angles = (positions + t).astype(F32) * frequency
        cosine, sine = jnp.cos(angles), jnp.sin(angles)
        rows += [jnp.concatenate([cosine, cosine]), jnp.concatenate([-sine, sine])]
    return jnp.stack(rows)


def per_device(
    inputs,
    positions,
    attn_gain,
    ffn_gain,
    qkv_weight,
    out_weight,
    gate_weight,
    up_weight,
    down_weight,
    k_cache,
    v_cache,
):
    gx, gy = lax.axis_index("gx"), lax.axis_index("gy")
    where = jnp.stack([gray(gx >> 2) * 4 + gray(gx & 3), gy]).astype(jnp.int32)
    angles = rotations(positions)
    attn_gain, ffn_gain = attn_gain.reshape(1, WIDTH), ffn_gain.reshape(1, WIDTH)

    twin = swap_gy(out_weight, 1)
    residual, near, far, attn_gain, qkv_weight, out_weight = gather_rows(
        inputs.reshape(32, WIDTH), attn_gain, qkv_weight, out_weight
    )
    partial = qkv_partial(where, near, far, attn_gain, qkv_weight, angles, twin)
    partial = partial.reshape(128, 24, HD)
    received = lax.all_to_all(partial, ("gx", "gy"), 0, 0, tiled=True).reshape(NX, NY, 24, HD)
    attended, new_kv = attend(angles, received, k_cache, v_cache)
    heads = lax.all_to_all(
        attended.reshape(64, 32, HD),
        ("gx", "gy"),
        0,
        0,
        axis_index_groups=[[i * NY + 2 * j + core for i in range(NX) for j in range(NY // 2)] for core in range(2)],
        tiled=True,
    )
    even_odd = sum_over_x(*out_partial(where, heads.reshape(64 * 32, HD), out_weight, twin))
    after_attn, lhs, *sends = send_partial(
        where, residual, far, attn_gain, ffn_gain, even_odd, gate_weight, up_weight
    )
    units = hidden_units(lhs, ffn_gain, gate_weight, up_weight, sends)
    outputs = add_ffn(after_attn, *down_partial(where, units, down_weight))
    return outputs.reshape(2, 16, WIDTH), new_kv


def solution(mesh):
    placed = (
        P(None, "gy", "gx"),
        P(("gx", "gy")),
        P("gx"),
        P("gx"),
        P("gx", "gy"),
        P("gy", "gx"),
        P("gx", "gy"),
        P("gx", "gy"),
        P("gy", "gx"),
        P(("gx", "gy"), None, None, None),
        P(("gx", "gy"), None, None, None),
    )
    return jax.shard_map(
        per_device,
        mesh=mesh,
        in_specs=placed,
        out_specs=(P(None, "gy", "gx"), P(("gx", "gy"), None, None, None)),
        check_vma=False,
    )
```
